32 devices in a mesh: dp: 4 (over y, x), expert: 8 (over z, core).
Axes of the slice: x: 2, y: 2, z: 4, core: 2. Of those that a mesh axis runs over, the one named last changes fastest.
Arguments:
- tokens: bfloat16 [4096, 1024], P(('dp', 'expert')), may hold values from -6 to 6
- upstream: bfloat16 [4096, 1024], P(('dp', 'expert')), may hold values from -6 to 6
- task_ids: int32 [4096, 1], P(('dp', 'expert')), may hold values from 0 to 7; in each aligned block of 128 rows (0 to 127, 128 to 255, ...) at most 18 rows name the same one
- task_expert: int32 [8], replicated, may hold values from 0 to 7, each once
- w_in: bfloat16 [8, 1024, 4096], P('expert', None, 'dp'), may hold values from -0.1875 to 0.1875
- w_out: bfloat16 [8, 4096, 1024], P('expert', 'dp'), may hold values from -0.09375 to 0.09375
Outputs:
- token_grad: bfloat16 [4096, 1024], P(('dp', 'expert'))
- grad_in: float32 [8, 1024, 4096], P('expert', None, 'dp')
- grad_out: float32 [8, 4096, 1024], P('expert', 'dp')
The draws below stay inside these ranges and needn't reach their ends.
Inputs may be any that keep to these rules, and one draw needn't show every extreme that they name: `task_ids`: among the 128 rows of one device no task appears more than 18 times, and some task appears exactly 18 times in the rows of some device. `task_expert`: each expert is the expert of exactly one task.
All inputs are finite; a program needn't handle non-finite values.
Results may differ from the reference program's by a relative error of at most 0.023.
Values may be sent and summed in bfloat16 or wider, within the bound.
A program may use at most 64 MiB of HBM per device.

```python
import math
import jax
import jax.numpy as jnp
import numpy as np
from jax import lax

D = 1024
FF = 4096
TOK_DEV = 128
EXPERTS = 8
CAP = 18
FF_DEV = 1024
TOKENS = 4096
N_DP = 4
N_EXPERT = 8


def shard_levels(rng, dims, split, least, top_value):
    def one(axis_at, parts):
        steps = jax.random.uniform(jax.random.fold_in(jax.random.fold_in(rng, 6), axis_at), (parts,), jnp.float32, least / len(split), top_value / len(split))
        return jnp.repeat(jnp.exp(steps), dims[axis_at] // parts).reshape((-1,) + (1,) * (len(dims) - axis_at - 1))

    factor_of = one(*split[0])
    for cut in split[1:]:
        factor_of = factor_of * one(*cut)
    return factor_of


def assign_block(key, own, number, rows, number_of, top, limit, lean):
    sequence = jax.random.permutation(key, number_of)
    heavy_load, ordinary = load_shares(number_of, rows * top, limit, lean, True), load_shares(number_of, rows * top, limit, lean, False)
    places = jnp.arange(number_of)

    def named(sizes, offset_by):
        used = int((sizes > 0).sum())
        fixed = max(1, used // 4)
        shifted = fixed + (places - fixed + offset_by * (used - fixed)) % max(1, number_of - fixed)
        return jnp.zeros((number_of,), jnp.int32).at[sequence[jnp.where(places < fixed, places, shifted)]].set(jnp.asarray(sizes, jnp.int32))

    sizes = jnp.where(number % 4 == 0, named(heavy_load, number // 4), named(ordinary, number - number // 4 - 1))
    mixed = jax.random.permutation(jax.random.fold_in(own, 3), number_of)
    giver, sink = mixed[0:number_of // 2 * 2:2], mixed[1:number_of // 2 * 2:2]
    slack = jnp.minimum(sizes[giver] - 1, limit - sizes[sink]) // 2
    slack = jnp.where((giver == sequence[0]) | (sink == sequence[0]) | (sizes[sink] == 0), 0, jnp.maximum(slack, 0))
    shifted = jax.random.randint(jax.random.fold_in(own, 4), (number_of // 2,), 0, 1 << 20) % (slack + 1)
    sizes = sizes.at[giver].add(-shifted).at[sink].add(shifted)
    labels = jnp.searchsorted(jnp.cumsum(sizes), jnp.arange(rows * top), side="right").astype(jnp.int32)
    grid = labels.reshape(top, rows).T
    grid = grid[jax.random.permutation(jax.random.fold_in(own, 1), rows)]
    offset_by = jax.random.randint(jax.random.fold_in(own, 2), (rows, 1), 0, top)
    return jnp.take_along_axis(grid, (jnp.arange(top)[None, :] + offset_by) % top, axis=1)


def load_shares(amount, total, bound, skew, full):
    weights = [(1 << 20) // math.isqrt(grade ** skew) + 1 for grade in range(1, amount + 1)]
    largest = bound if full else min(bound, max(-(-total // amount), total * weights[0] // sum(weights)))
    least = 1 if total - largest >= amount - 1 else 0
    given, surplus = [largest] + [least] * (amount - 1), total - largest - least * (amount - 1)
    while surplus > 0:
        movable = [i for i in range(1, amount) if given[i] < largest] or [i for i in range(1, amount) if given[i] < bound]
        pool, left = sum([weights[i] for i in movable]), surplus
        for i in movable:
            addition = min(bound - given[i], max(1, left * weights[i] // pool), surplus)
            given[i] = given[i] + addition
            surplus = surplus - addition
    return np.array(given)


def noise(stream_key, shape, scale, bound, cuts=(), kind=jnp.bfloat16):
    values = scale * jax.random.normal(stream_key, shape, jnp.float32)
    if cuts:
        values = values * shard_levels(stream_key, shape, cuts, -0.22, 0.18)
    return jnp.clip(values, -bound, bound).astype(kind)


def setup_inputs(seed: int = 0) -> dict:
    arg_keys = jax.random.split(jax.random.key(seed), 7)
    tokens = noise(arg_keys[0], (TOKENS, D), 1.0, 6.0, ((0, 32),))
    upstream = noise(arg_keys[1], (TOKENS, D), 1.0, 6.0, ((0, 32),))
    task_ids_keys = jax.random.split(jax.random.fold_in(arg_keys[2], 1), TOKENS // TOK_DEV)
    task_ids_turns = jax.random.permutation(jax.random.fold_in(arg_keys[2], 3), TOKENS // TOK_DEV)
    task_ids = jax.vmap(lambda own, number: assign_block(jax.random.fold_in(arg_keys[2], 2), own, number, TOK_DEV, EXPERTS, 1, CAP, 2))(task_ids_keys, task_ids_turns).reshape((TOKENS, 1))
    task_expert = jax.random.permutation(arg_keys[3], EXPERTS).astype(jnp.int32)
    w_in = noise(arg_keys[4], (EXPERTS, D, FF), D ** -0.5, 0.1875, ((0, 8), (2, 4)))
    w_out = noise(arg_keys[5], (EXPERTS, FF, D), FF ** -0.5, 0.09375, ((0, 8), (1, 4)))
    return dict(tokens=tokens, upstream=upstream, task_ids=task_ids, task_expert=task_expert, w_in=w_in, w_out=w_out)


coeff = 0.7978845608028654


def gelu_pair(pre):
    inner = coeff * (pre + 0.044715 * pre * pre * pre)
    tanh_val = jnp.tanh(inner)
    act = 0.5 * pre * (1.0 + tanh_val)
    slope = 0.5 * (1.0 + tanh_val) + 0.5 * pre * (1.0 - tanh_val * tanh_val) * coeff * (1.0 + 3.0 * 0.044715 * pre * pre)
    return act, slope


def reference(tokens, upstream, task_ids, task_expert, w_in, w_out):
    route = task_expert[task_ids[:, 0]].astype(jnp.int32)
    order = jnp.argsort(route, stable=True).astype(jnp.int32)
    hot = (route[:, None] == jnp.arange(EXPERTS, dtype=jnp.int32)[None, :]).astype(jnp.int32)
    counts = jnp.sum(hot, axis=0).astype(jnp.int32)
    offsets = (jnp.cumsum(counts) - counts).astype(jnp.int32)
    most_rows = N_DP * N_EXPERT * CAP
    padded_tokens = jnp.concatenate([tokens, jnp.zeros((1, D), tokens.dtype)], axis=0)
    padded_grads = jnp.concatenate([upstream, jnp.zeros((1, D), upstream.dtype)], axis=0)
    padded_order = jnp.concatenate([order, jnp.zeros((most_rows,), jnp.int32)], axis=0)
    steps_idx = jnp.arange(most_rows, dtype=jnp.int32)

    def one_expert(expert):
        start = offsets[expert]
        picked = lax.dynamic_slice_in_dim(padded_order, start, most_rows, 0)
        index = jnp.where(steps_idx < counts[expert], picked, jnp.int32(TOKENS)).astype(jnp.int32)
        rows = padded_tokens[index]
        grads = padded_grads[index]
        first = w_in[expert]
        second = w_out[expert]
        pre = jnp.dot(rows, first, preferred_element_type=jnp.float32)
        act, slope = gelu_pair(pre)
        act = act.astype(jnp.bfloat16)
        grad_second = jnp.dot(act.T, grads, preferred_element_type=jnp.float32)
        dact = jnp.dot(grads, second.T, preferred_element_type=jnp.float32)
        dpre = (dact * slope).astype(jnp.bfloat16)
        grad_first = jnp.dot(rows.T, dpre, preferred_element_type=jnp.float32)
        total = jnp.zeros((most_rows, D), jnp.float32)
        for block in range(N_DP):
            low = block * FF_DEV
            piece = jnp.dot(dpre[:, low:low + FF_DEV], first[:, low:low + FF_DEV].T, preferred_element_type=jnp.float32)
            total = total + piece.astype(jnp.bfloat16).astype(jnp.float32)
        return total.astype(jnp.bfloat16), index, grad_first, grad_second

    results, indices, grad_in, grad_out = lax.map(one_expert, jnp.arange(EXPERTS, dtype=jnp.int32))
    token_grad = jnp.zeros((TOKENS + 1, D), jnp.bfloat16)
    token_grad = token_grad.at[indices.reshape(-1)].set(results.reshape(-1, D))
    return token_grad[:TOKENS], grad_in, grad_out
```

```python
import functools

import jax
import jax.numpy as jnp
from jax import lax
from jax.experimental import pallas as pl
from jax.experimental.pallas import tpu as pltpu
from jax.sharding import PartitionSpec as P

coeff = 0.7978845608028654
MESH = pl.DeviceIdType.MESH
BF = jnp.bfloat16
F32 = jnp.float32
MAIN = 16
LANES = 128


def gelu_pair(pre):
    inner = coeff * (pre + 0.044715 * pre * pre * pre)
    tanh_val = jnp.tanh(inner)
    act = 0.5 * pre * (1.0 + tanh_val)
    slope = 0.5 * (1.0 + tanh_val) + 0.5 * pre * (1.0 - tanh_val * tanh_val) * coeff * (
        1.0 + 3.0 * 0.044715 * pre * pre
    )
    return (act, slope)


def fold(rows, width):
    return jnp.concatenate([rows[:, c : c + LANES] for c in range(0, width, LANES)], axis=0)


def unfold(rows, start, width):
    return jnp.concatenate(
        [rows[c * MAIN : (c + 1) * MAIN, start : start + LANES] for c in range(width // LANES)], axis=1
    )


def exchange_kernel(
    n_expert,
    rows_dev,
    width,
    ff,
    tokens_ref,
    upstream_ref,
    ids_ref,
    experts_ref,
    first_hbm,
    second_hbm,
    out_ref,
    xg_hbm,
    ad_hbm,
    first,
    second,
    send,
    got,
    extra,
    ad,
    part,
    peer,
    back_send,
    back_got,
    w_sem,
    z_send,
    x_send,
    y_send,
    f_send,
    recv,
    p_send,
    p_recv,
    b_send,
    b_recv,
    o_sem,
):
    chips = n_expert // 2
    group = n_expert * MAIN
    over = MAIN
    chunk = group + over
    e = lax.axis_index("expert")
    d = lax.axis_index("dp")
    chip, core = lax.div(e, 2), lax.rem(e, 2)
    xn = d + 1 - 2 * lax.rem(d, 2)
    yn = lax.rem(d + 2, 4)
    diag = lax.rem(xn + 2, 4)

    def target(i):
        return lax.rem(chip + i // 2, chips) * 2 + lax.rem(core + i % 2, 2)

    def source(i):
        return lax.rem(chip + chips - i // 2, chips) * 2 + lax.rem(core + i % 2, 2)

    def block(index):
        return pl.ds(pl.multiple_of(index * MAIN, MAIN), MAIN)

    def at(k, s):
        return pl.ds(pl.multiple_of(k * group + s * MAIN, MAIN), MAIN)

    barrier = pltpu.get_barrier_semaphore()
    for i in range(1, n_expert):
        pl.semaphore_signal(barrier, inc=1, device_id={"expert": target(i)}, device_id_type=MESH)
    for near in (xn, yn, diag):
        pl.semaphore_signal(barrier, inc=1, device_id={"dp": near}, device_id_type=MESH)

    loads = [
        pltpu.make_async_copy(first_hbm, first, w_sem.at[0]),
        pltpu.make_async_copy(second_hbm, second, w_sem.at[1]),
    ]
    for load in loads:
        load.start()

    lane8 = lax.broadcasted_iota(jnp.int32, (rows_dev, n_expert), 1)
    hot = (ids_ref[...] == lane8).astype(F32)
    goal = jnp.sum(hot * experts_ref[...].astype(F32), axis=1, keepdims=True)
    row = lax.broadcasted_iota(jnp.int32, (rows_dev, rows_dev), 0)
    col = lax.broadcasted_iota(jnp.int32, (rows_dev, rows_dev), 1)
    lane = col.astype(F32)
    dest = (goal == lane).astype(F32)
    before = jnp.dot((row > col).astype(BF), dest.astype(BF), preferred_element_type=F32)
    rank = jnp.sum(before * dest, axis=1, keepdims=True)
    is_main = (rank < MAIN).astype(F32)
    main_hot = ((goal * MAIN + rank == lane).astype(F32) * is_main).astype(BF)
    over_hot = ((goal * 2 + (rank - MAIN) == lane).astype(F32) * (1.0 - is_main)).astype(BF)
    turned = (row >> 1 & 7) * 16 + (row >> 4) * 2 + (row & 1)
    perm = (turned == col).astype(BF)

    def gather(hot_rows, values):
        return lax.dot_general(
            hot_rows, values, (((0,), (0,)), ((), ())), preferred_element_type=F32
        ).astype(BF)

    tokens = tokens_ref[...]
    upstream = upstream_ref[...]
    send[:, :width] = gather(main_hot, tokens)
    send[:, width : 2 * width] = gather(main_hot, upstream)
    folded = jnp.concatenate(
        [
            fold(gather(over_hot, tokens)[:over], width),
            fold(gather(over_hot, upstream)[:over], width),
        ],
        axis=1,
    )
    send[:, 2 * width :] = jnp.dot(perm, folded, preferred_element_type=F32).astype(BF)

    pl.semaphore_wait(barrier, n_expert - 1 + 3)

    started = []

    def push(src, dst, send_sem, recv_sem, device):
        copy = pltpu.make_async_remote_copy(
            src_ref=src,
            dst_ref=dst,
            send_sem=send_sem,
            recv_sem=recv_sem,
            device_id=device,
            device_id_type=MESH,
        )
        copy.start()
        started.append(copy)

    for i in range(1, n_expert):
        push(send.at[block(target(i))], got.at[at(0, e)], z_send.at[i - 1], recv.at[e], {"expert": target(i)})
    got[at(0, e), :] = send[block(e), :]

    def arrived(k, s):
        here = got.at[at(k, s)]
        pltpu.make_async_copy(here, here, recv.at[k * n_expert + s]).wait()

    def forward(i):
        s = source(i)
        arrived(1, s)
        arrived(2, s)
        if i % 2 == 0:
            push(got.at[at(1, s)], got.at[at(3, s)], f_send.at[i], recv.at[3 * n_expert + s], {"dp": yn})
        else:
            push(got.at[at(2, s)], got.at[at(3, s)], f_send.at[i], recv.at[3 * n_expert + s], {"dp": xn})

    lag = 2
    for i in range(n_expert):
        s = source(i)
        if i > 0:
            arrived(0, s)
        push(got.at[at(0, s)], got.at[at(1, s)], x_send.at[i], recv.at[n_expert + s], {"dp": xn})
        push(got.at[at(0, s)], got.at[at(2, s)], y_send.at[i], recv.at[2 * n_expert + s], {"dp": yn})
        if i >= lag:
            forward(i - lag)
    for i in range(n_expert - lag, n_expert):
        forward(i)
    for load in loads:
        load.wait()

    outs = []

    def ship(src, dst):
        copy = pltpu.make_async_copy(src, dst, o_sem.at[len(outs)])
        copy.start()
        outs.append(copy)

    tile = 256

    def work(k):
        main = pl.ds(k * group, group)
        rest = pl.ds(k * over, over)
        mine = pl.ds(k * chunk, chunk)
        open_rows = jnp.dot(perm, got[main, 2 * width :], preferred_element_type=F32).astype(BF)
        extra[rest, :width] = unfold(open_rows, 0, width)
        extra[rest, width:] = unfold(open_rows, LANES, width)

        @pl.loop(0, ff // tile)
        def _(f):
            cols = pl.ds(pl.multiple_of(f * tile, tile), tile)
            later = pl.ds(pl.multiple_of(ff + f * tile, tile), tile)
            rows = jnp.concatenate([got[main, :width], extra[rest, :width]], axis=0)
            grads = jnp.concatenate([got[main, width : 2 * width], extra[rest, width:]], axis=0)
            pre = jnp.dot(rows, first[:, cols], preferred_element_type=F32)
            act, slope = gelu_pair(pre)
            ad[mine, cols] = act.astype(BF)
            dact = lax.dot_general(
                grads, second[cols, :], (((1,), (1,)), ((), ())), preferred_element_type=F32
            )
            ad[mine, later] = (dact * slope).astype(BF)

        @pl.loop(0, width // tile)
        def _(f):
            cols = pl.ds(pl.multiple_of(f * tile, tile), tile)
            part[mine, cols] = lax.dot_general(
                ad[mine, ff:], first[cols, :], (((1,), (1,)), ((), ())), preferred_element_type=F32
            ).astype(BF)

        ship(got.at[main, pl.ds(0, 2 * width)], xg_hbm.at[pl.ds(k * chunk, group)])
        ship(extra.at[rest], xg_hbm.at[pl.ds(k * chunk + group, over)])
        ship(ad.at[mine], ad_hbm.at[mine])

    def give(k, near):
        push(
            part.at[pl.ds(k * chunk, chunk)],
            peer.at[pl.ds((k - 1) * chunk, chunk)],
            p_send.at[k - 1],
            p_recv.at[k - 1],
            {"dp": near},
        )

    work(1)
    give(1, xn)
    work(2)
    give(2, yn)
    for i in range(n_expert):
        arrived(3, source(i))
    work(3)
    give(3, diag)
    work(0)

    for k in range(3):
        here = peer.at[pl.ds(k * chunk, chunk)]
        pltpu.make_async_copy(here, here, p_recv.at[k]).wait()

    def total(low, size):
        value = part[low : low + size, :].astype(F32)
        for k in range(3):
            value = value + peer[k * chunk + low : k * chunk + low + size, :].astype(F32)
        return value.astype(BF)

    back_send[:, :width] = total(0, group)
    back_send[:, width:] = jnp.dot(
        perm, fold(total(group, over), width), preferred_element_type=F32
    ).astype(BF)
    for i in range(1, n_expert):
        push(
            back_send.at[block(target(i))],
            back_got.at[block(e)],
            b_send.at[i - 1],
            b_recv.at[e],
            {"expert": target(i)},
        )
    back_got[block(e), :] = back_send[block(e), :]
    for i in range(1, n_expert):
        s = source(i)
        here = back_got.at[block(s)]
        pltpu.make_async_copy(here, here, b_recv.at[s]).wait()
    open_rows = jnp.dot(perm, back_got[:, width:], preferred_element_type=F32).astype(BF)
    extra_rows = unfold(open_rows, 0, width)
    result = jnp.dot(main_hot, back_got[:, :width], preferred_element_type=F32)
    result = result + jnp.dot(over_hot[:, :over], extra_rows, preferred_element_type=F32)
    out_ref[...] = result.astype(BF)
    for copy in started:
        copy.wait_send()
    for copy in outs:
        copy.wait()


def weight_kernel(x_tile, grads, act_tile, dpre, grad_in, grad_out):
    spec = (((0,), (0,)), ((), ()))
    grad_in[...] = lax.dot_general(x_tile[...], dpre[...], spec, preferred_element_type=F32)
    grad_out[...] = lax.dot_general(act_tile[...], grads[...], spec, preferred_element_type=F32)


def fused_body(tokens, upstream, task_ids, task_expert, w_in, w_out):
    n_expert = lax.axis_size("expert")
    rows_dev, width = tokens.shape
    ff = w_in.shape[2]
    group = n_expert * MAIN
    chunk = group + MAIN
    rows = 4 * chunk
    first, second = w_in[0], w_out[0]
    dma = pltpu.SemaphoreType.DMA
    vmem = pl.BlockSpec(memory_space=pltpu.VMEM)
    hbm = pl.BlockSpec(memory_space=pl.ANY)
    token_grad, xg, ad = pl.pallas_call(
        functools.partial(exchange_kernel, n_expert, rows_dev, width, ff),
        out_shape=(
            jax.ShapeDtypeStruct((rows_dev, width), BF),
            jax.ShapeDtypeStruct((rows, 2 * width), BF),
            jax.ShapeDtypeStruct((rows, 2 * ff), BF),
        ),
        in_specs=[vmem, vmem, vmem, vmem, hbm, hbm],
        out_specs=(vmem, hbm, hbm),
        scratch_shapes=[
            pltpu.VMEM((width, ff), BF),
            pltpu.VMEM((ff, width), BF),
            pltpu.VMEM((group, 2 * width + 2 * LANES), BF),
            pltpu.VMEM((4 * group, 2 * width + 2 * LANES), BF),
            pltpu.VMEM((4 * MAIN, 2 * width), BF),
            pltpu.VMEM((rows, 2 * ff), BF),
            pltpu.VMEM((rows, width), BF),
            pltpu.VMEM((3 * chunk, width), BF),
            pltpu.VMEM((group, width + LANES), BF),
            pltpu.VMEM((group, width + LANES), BF),
            dma((2,)),
            dma((n_expert - 1,)),
            dma((n_expert,)),
            dma((n_expert,)),
            dma((n_expert,)),
            dma((4 * n_expert,)),
            dma((3,)),
            dma((3,)),
            dma((n_expert - 1,)),
            dma((n_expert,)),
            dma((12,)),
        ],
        compiler_params=pltpu.CompilerParams(
            collective_id=0, has_side_effects=True, vmem_limit_bytes=40 * 1024 * 1024
        ),
        cost_estimate=pl.CostEstimate(
            flops=6 * rows * width * ff, bytes_accessed=12 * width * ff, transcendentals=rows * ff
        ),
    )(tokens, upstream, task_ids, task_expert.reshape(1, -1), first, second)
    tile = 256
    grad_in, grad_out = pl.pallas_call(
        weight_kernel,
        grid=(width // tile,),
        out_shape=(
            jax.ShapeDtypeStruct((width, ff), F32),
            jax.ShapeDtypeStruct((ff, width), F32),
        ),
        in_specs=[
            pl.BlockSpec((rows, tile), lambda i: (0, i)),
            pl.BlockSpec((rows, width), lambda i: (0, 1)),
            pl.BlockSpec((rows, tile), lambda i: (0, i)),
            pl.BlockSpec((rows, ff), lambda i: (0, 1)),
        ],
        out_specs=(
            pl.BlockSpec((tile, ff), lambda i: (i, 0)),
            pl.BlockSpec((tile, width), lambda i: (i, 0)),
        ),
        compiler_params=pltpu.CompilerParams(vmem_limit_bytes=40 * 1024 * 1024),
        cost_estimate=pl.CostEstimate(
            flops=4 * rows * width * ff, bytes_accessed=16 * width * ff, transcendentals=0
        ),
    )(xg, xg, ad, ad)
    return (token_grad, grad_in[None], grad_out[None])


def general_body(tokens, upstream, task_ids, task_expert, w_in, w_out):
    n_expert = lax.axis_size("expert")
    rows_dev = tokens.shape[0]
    width = tokens.shape[1]
    experts = task_expert.shape[0]
    capacity = max(2, (9 * rows_dev // 8 + n_expert - 1) // n_expert)
    lanes = jnp.arange(experts, dtype=jnp.int32)
    task_hot = (task_ids == lanes[None, :]).astype(jnp.int32)
    target = jnp.sum(task_hot * task_expert[None, :], axis=1)
    dest_hot = (target[:, None] == lanes[None, :]).astype(jnp.int32)
    before = jnp.cumsum(dest_hot, axis=0) - dest_hot
    rank = jnp.sum(before * dest_hot, axis=1)
    slot = target * capacity + rank
    packer = (jnp.arange(experts * capacity, dtype=jnp.int32)[:, None] == slot[None, :]).astype(
        jnp.bfloat16
    )
    send_rows = (
        jnp.dot(packer, tokens, preferred_element_type=jnp.float32)
        .astype(jnp.bfloat16)
        .reshape(experts, capacity, width)
    )
    send_grads = (
        jnp.dot(packer, upstream, preferred_element_type=jnp.float32)
        .astype(jnp.bfloat16)
        .reshape(experts, capacity, width)
    )
    first = w_in[0]
    second = w_out[0]
    got_rows, got_grads = (
        lax.all_to_all(send_rows, "expert", split_axis=0, concat_axis=0, tiled=True),
        lax.all_to_all(send_grads, "expert", split_axis=0, concat_axis=0, tiled=True),
    )
    got_rows = got_rows.reshape(experts * capacity, width)
    got_grads = got_grads.reshape(experts * capacity, width)
    all_rows, all_grads = (
        lax.all_gather(got_rows, "dp", axis=0, tiled=True),
        lax.all_gather(got_grads, "dp", axis=0, tiled=True),
    )
    pre = jnp.dot(all_rows, first, preferred_element_type=jnp.float32)
    act, slope = gelu_pair(pre)
    act = act.astype(jnp.bfloat16)
    grad_second = lax.dot_general(
        act, all_grads, (((0,), (0,)), ((), ())), preferred_element_type=jnp.float32
    )
    dact = lax.dot_general(
        all_grads, second, (((1,), (1,)), ((), ())), preferred_element_type=jnp.float32
    )
    dpre = (dact * slope).astype(jnp.bfloat16)
    grad_first = lax.dot_general(
        all_rows, dpre, (((0,), (0,)), ((), ())), preferred_element_type=jnp.float32
    )
    partial_value = lax.dot_general(
        dpre, first, (((1,), (1,)), ((), ())), preferred_element_type=jnp.float32
    )
    own = lax.psum_scatter(
        partial_value.astype(jnp.bfloat16), "dp", scatter_dimension=0, tiled=True
    ).astype(jnp.float32)
    own = own.astype(jnp.bfloat16).reshape(experts, capacity, width)
    back = lax.all_to_all(own, "expert", split_axis=0, concat_axis=0, tiled=True).reshape(
        experts * capacity, width
    )
    token_grad = lax.dot_general(
        packer, back, (((0,), (0,)), ((), ())), preferred_element_type=jnp.float32
    ).astype(jnp.bfloat16)
    return (token_grad, grad_first[None], grad_second[None])


def body(mesh, tokens, upstream, task_ids, task_expert, w_in, w_out):
    n_expert = mesh.shape["expert"]
    rows_dev, width = tokens.shape
    ff = w_in.shape[2]
    capacity = max(2, (9 * rows_dev // 8 + n_expert - 1) // n_expert)
    fits = (
        mesh.shape["dp"] == 4
        and n_expert == 8
        and rows_dev == 128
        and capacity <= MAIN + 2
        and width == n_expert * LANES
        and ff == width
    )
    run = fused_body if fits else general_body
    return run(tokens, upstream, task_ids, task_expert, w_in, w_out)


def solution(mesh):
    placed = (
        P(("dp", "expert"), None),
        P(("dp", "expert"), None),
        P(("dp", "expert"), None),
        P(),
        P("expert", None, "dp"),
        P("expert", "dp", None),
    )
    return jax.shard_map(
        functools.partial(body, mesh),
        mesh=mesh,
        in_specs=placed,
        out_specs=(P(("dp", "expert"), None), P("expert", None, "dp"), P("expert", "dp", None)),
        check_vma=False,
    )
```

```python
import functools

import jax
import jax.numpy as jnp
from jax import lax
from jax.experimental import pallas as pl
from jax.experimental.pallas import tpu as pltpu
from jax.sharding import PartitionSpec as P

coeff = 0.7978845608028654
MESH = pl.DeviceIdType.MESH
BF = jnp.bfloat16
F32 = jnp.float32
MAIN = 16
LANES = 128


def gelu_pair(pre):
    square = pre * pre
    tanh_val = jnp.tanh(pre * (coeff + coeff * 0.044715 * square))
    half = 0.5 + 0.5 * tanh_val
    slope = half + half * (1.0 - tanh_val) * (pre * (coeff + 3.0 * 0.044715 * coeff * square))
    return (pre * half, slope)


def fold(rows, width):
    return jnp.concatenate([rows[:, c : c + LANES] for c in range(0, width, LANES)], axis=0)


def unfold(rows, start, width):
    return jnp.concatenate(
        [rows[c * MAIN : (c + 1) * MAIN, start : start + LANES] for c in range(width // LANES)], axis=1
    )


def exchange_kernel(
    n_expert,
    rows_dev,
    width,
    ff,
    tokens_hbm,
    upstream_hbm,
    ids_hbm,
    experts_ref,
    first_hbm,
    second_hbm,
    out_ref,
    grad_in_out,
    grad_out_out,
    tokens_ref,
    upstream_ref,
    ids_ref,
    first,
    second,
    send,
    got,
    extra,
    ad,
    part,
    peer,
    grad_in,
    grad_out,
    back_send,
    back_got,
    w_sem,
    z_send,
    x_send,
    y_send,
    f_send,
    recv,
    p_send,
    p_recv,
    b_send,
    b_recv,
    o_sem,
):
    chips = n_expert // 2
    group = n_expert * MAIN
    over = MAIN
    half = group // 2
    mains = 4 * group
    e = lax.axis_index("expert")
    d = lax.axis_index("dp")
    chip, core = lax.div(e, 2), lax.rem(e, 2)
    xn = d + 1 - 2 * lax.rem(d, 2)
    yn = lax.rem(d + 2, 4)
    diag = lax.rem(xn + 2, 4)
    upper = lax.div(chip, chips // 2)
    inner = chip + upper * (chips - 1 - 2 * chip)

    def order(i):
        place = (inner, 1 - inner, 2, 3)[i // 2]
        return (place + upper * (chips - 1 - 2 * place)) * 2 + lax.rem(core + i % 2, 2)

    def block(index):
        return pl.ds(pl.multiple_of(index * MAIN, MAIN), MAIN)

    def at(k, s):
        return pl.ds(pl.multiple_of(k * group + s * MAIN, MAIN), MAIN)

    loads = [
        pltpu.make_async_copy(src, dst, w_sem.at[i])
        for i, (src, dst) in enumerate(
            (
                (ids_hbm, ids_ref),
                (tokens_hbm, tokens_ref),
                (upstream_hbm, upstream_ref),
                (first_hbm, first),
                (second_hbm, second),
            )
        )
    ]
    for load in loads:
        load.start()

    barrier = pltpu.get_barrier_semaphore()
    for i in range(1, n_expert):
        pl.semaphore_signal(barrier, inc=1, device_id={"expert": order(i)}, device_id_type=MESH)
    for near in (xn, yn, diag):
        pl.semaphore_signal(barrier, inc=1, device_id={"dp": near}, device_id_type=MESH)

    row = lax.broadcasted_iota(jnp.int32, (rows_dev, rows_dev), 0)
    col = lax.broadcasted_iota(jnp.int32, (rows_dev, rows_dev), 1)
    line = row.astype(F32)
    earlier = (row < col).astype(BF)
    turned = (row >> 1 & 7) * 16 + (row >> 4) * 2 + (row & 1)
    perm = (turned == col).astype(BF)
    loads[0].wait()
    ids = ids_ref[...]
    goal = jnp.zeros(ids.shape, F32)
    for k in range(n_expert):
        goal = jnp.where(ids == k, experts_ref[k].astype(F32), goal)
    dest = (goal == line).astype(F32)
    before = jnp.dot(dest.astype(BF), earlier, preferred_element_type=F32)
    rank = jnp.sum(before * dest, axis=0, keepdims=True)
    is_main = (rank < MAIN).astype(F32)
    main_hot = ((goal * MAIN + rank == line).astype(F32) * is_main).astype(BF)
    over_hot = ((goal * 2 + (rank - MAIN) == line).astype(F32) * (1.0 - is_main)).astype(BF)[:over]

    def pick(hot_rows, values):
        return jnp.dot(hot_rows, values, preferred_element_type=F32).astype(BF)

    loads[1].wait()
    tokens = tokens_ref[...]
    send[:, :width] = pick(main_hot, tokens)
    loads[2].wait()
    upstream = upstream_ref[...]
    send[:, width : 2 * width] = pick(main_hot, upstream)
    folded = jnp.concatenate(
        [fold(pick(over_hot, tokens), width), fold(pick(over_hot, upstream), width)], axis=1
    )
    send[:, 2 * width :] = pick(perm, folded)

    pl.semaphore_wait(barrier, n_expert - 1 + 3)

    started = []

    def push(src, dst, send_sem, recv_sem, device):
        copy = pltpu.make_async_remote_copy(
            src_ref=src,
            dst_ref=dst,
            send_sem=send_sem,
            recv_sem=recv_sem,
            device_id=device,
            device_id_type=MESH,
        )
        copy.start()
        started.append(copy)

    def landed(here, sem):
        pltpu.make_async_copy(here, here, sem).wait()

    for i in range(1, n_expert):
        t = order(i)
        push(send.at[block(t)], got.at[at(0, e)], z_send.at[i - 1], recv.at[e], {"expert": t})
    got[at(0, e), :] = send[block(e), :]

    def arrived(k, s):
        landed(got.at[at(k, s)], recv.at[k * n_expert + s])

    def forward(i):
        s = order(i)
        arrived(1, s)
        arrived(2, s)
        if i % 2 == 0:
            push(got.at[at(1, s)], got.at[at(3, s)], f_send.at[i], recv.at[3 * n_expert + s], {"dp": yn})
        else:
            push(got.at[at(2, s)], got.at[at(3, s)], f_send.at[i], recv.at[3 * n_expert + s], {"dp": xn})

    lag = 2
    for i in range(n_expert):
        s = order(i)
        if i > 0:
            arrived(0, s)
        push(got.at[at(0, s)], got.at[at(1, s)], x_send.at[i], recv.at[n_expert + s], {"dp": xn})
        push(got.at[at(0, s)], got.at[at(2, s)], y_send.at[i], recv.at[2 * n_expert + s], {"dp": yn})
        if i >= lag:
            forward(i - lag)
    for i in range(n_expert - lag, n_expert):
        forward(i)
    for load in loads[3:]:
        load.wait()

    tile = 256

    def work(k, n):
        main = pl.ds(k * group, n * group)
        rest = pl.ds(k * over, n * over)
        tail = pl.ds(mains + k * over, n * over)
        cut = n * group
        for c in range(k, k + n):
            opened = pick(perm, got[pl.ds(c * group, group), 2 * width :])
            extra[pl.ds(c * over, over), :width] = unfold(opened, 0, width)
            extra[pl.ds(c * over, over), width:] = unfold(opened, LANES, width)

        @pl.loop(0, ff // tile)
        def _(f):
            cols = pl.ds(pl.multiple_of(f * tile, tile), tile)
            later = pl.ds(pl.multiple_of(ff + f * tile, tile), tile)
            rows = jnp.concatenate([got[main, :width], extra[rest, :width]], axis=0)
            grads = jnp.concatenate([got[main, width : 2 * width], extra[rest, width:]], axis=0)
            pre = jnp.dot(rows, first[:, cols], preferred_element_type=F32)
            act, slope = gelu_pair(pre)
            act = act.astype(BF)
            ad[main, cols] = act[:cut]
            ad[tail, cols] = act[cut:]
            dact = lax.dot_general(
                grads, second[cols, :], (((1,), (1,)), ((), ())), preferred_element_type=F32
            )
            dpre = (dact * slope).astype(BF)
            ad[main, later] = dpre[:cut]
            ad[tail, later] = dpre[cut:]

        @pl.loop(0, width // tile)
        def _(f):
            cols = pl.ds(pl.multiple_of(f * tile, tile), tile)
            dpre = jnp.concatenate([ad[main, ff:], ad[tail, ff:]], axis=0)
            value = lax.dot_general(
                dpre, first[cols, :], (((1,), (1,)), ((), ())), preferred_element_type=F32
            ).astype(BF)
            part[main, cols] = value[:cut]
            part[tail, cols] = value[cut:]

    far = (1 - upper) * half
    near = upper * half

    def spans(k):
        return (
            pl.ds(pl.multiple_of(k * group + far, half), half),
            pl.ds(mains + k * over, over),
            pl.ds(pl.multiple_of(k * group + near, half), half),
        )

    def slots(k):
        base = (k - 1) * group
        return (
            pl.ds(pl.multiple_of(base + far, half), half),
            pl.ds(3 * group + (k - 1) * over, over),
            pl.ds(pl.multiple_of(base + near, half), half),
        )

    def give(k, device):
        for j, (src, dst) in enumerate(zip(spans(k), slots(k))):
            i = 3 * (k - 1) + j
            push(part.at[src], peer.at[dst], p_send.at[i], p_recv.at[i], {"dp": device})

    work(1, 2)
    give(1, xn)
    give(2, yn)
    for i in range(n_expert):
        arrived(3, order(i))
    work(3, 1)
    give(3, diag)
    work(0, 1)

    def weight_grad(left, left_at, right, right_at, grad, grad_hbm, sems):
        @pl.loop(0, width // tile)
        def _(f):
            cols = pl.ds(pl.multiple_of(left_at + f * tile, tile), tile)
            mine = pl.ds(pl.multiple_of(f * tile, tile), tile)
            tall = jnp.concatenate([left[0][pl.ds(0, mains), cols], left[1][left[2], cols]], axis=0)
            wide = jnp.concatenate(
                [
                    right[0][pl.ds(0, mains), right_at : right_at + width],
                    right[1][right[2], right_at : right_at + width],
                ],
                axis=0,
            )
            grad[mine, :] = lax.dot_general(
                tall, wide, (((0,), (0,)), ((), ())), preferred_element_type=F32
            )
            pltpu.make_async_copy(grad.at[mine], grad_hbm.at[mine], o_sem.at[sems + f]).start()

    rows_all = (got, extra, pl.ds(0, 4 * over))
    hidden_all = (ad, ad, pl.ds(mains, 4 * over))
    weight_grad(hidden_all, 0, rows_all, width, grad_out, grad_out_out, 0)

    def total(j):
        value = part[spans(0)[j], :].astype(F32)
        for k in range(1, 4):
            landed(peer.at[slots(k)[j]], p_recv.at[3 * (k - 1) + j])
            value = value + peer[slots(k)[j], :].astype(F32)
        return value.astype(BF)

    def give_back(i):
        t = order(i)
        push(back_send.at[block(t)], back_got.at[block(e)], b_send.at[i - 1], b_recv.at[e], {"expert": t})

    back_send[pl.ds(pl.multiple_of(far, half), half), :width] = total(0)
    back_send[:, width:] = pick(perm, fold(total(1), width))
    for i in range(n_expert // 2, n_expert):
        give_back(i)
    back_send[pl.ds(pl.multiple_of(near, half), half), :width] = total(2)
    for i in range(1, n_expert // 2):
        give_back(i)
    back_got[block(e), :] = back_send[block(e), :]

    weight_grad(rows_all, 0, hidden_all, ff, grad_in, grad_in_out, 4)

    for i in range(1, n_expert):
        s = order(i)
        landed(back_got.at[block(s)], b_recv.at[s])
    extra_rows = unfold(pick(perm, back_got[:, width:]), 0, width)
    spec = (((0,), (0,)), ((), ()))
    result = lax.dot_general(main_hot, back_got[:, :width], spec, preferred_element_type=F32)
    result = result + lax.dot_general(over_hot, extra_rows, spec, preferred_element_type=F32)
    out_ref[...] = result.astype(BF)
    for copy in started:
        copy.wait_send()
    for f in range(width // tile):
        mine = pl.ds(f * tile, tile)
        pltpu.make_async_copy(grad_out.at[mine], grad_out_out.at[mine], o_sem.at[f]).wait()
        pltpu.make_async_copy(grad_in.at[mine], grad_in_out.at[mine], o_sem.at[4 + f]).wait()


def deliver_kernel(first, second, first_out, second_out, sem):
    rows = first.shape[0] // 4
    copies = []
    for i in range(4):
        here = pl.ds(i * rows, rows)
        copies.append(pltpu.make_async_copy(first.at[here], first_out.at[here], sem.at[2 * i]))
        copies.append(pltpu.make_async_copy(second.at[here], second_out.at[here], sem.at[2 * i + 1]))
    for copy in copies:
        copy.start()
    for copy in copies:
        copy.wait()


def fused_body(tokens, upstream, task_ids, task_expert, w_in, w_out):
    n_expert = lax.axis_size("expert")
    rows_dev, width = tokens.shape
    ff = w_in.shape[2]
    group = n_expert * MAIN
    chunk = group + MAIN
    rows = 4 * chunk
    first, second = w_in[0], w_out[0]
    dma = pltpu.SemaphoreType.DMA
    vmem = pl.BlockSpec(memory_space=pltpu.VMEM)
    smem = pl.BlockSpec(memory_space=pltpu.SMEM)
    hbm = pl.BlockSpec(memory_space=pltpu.HBM)
    free = pl.BlockSpec(memory_space=pl.ANY)
    grads = (
        jax.ShapeDtypeStruct((width, ff), F32),
        jax.ShapeDtypeStruct((ff, width), F32),
    )
    token_grad, grad_in, grad_out = pl.pallas_call(
        functools.partial(exchange_kernel, n_expert, rows_dev, width, ff),
        out_shape=(jax.ShapeDtypeStruct((rows_dev, width), BF),) + grads,
        in_specs=[hbm, hbm, hbm, smem, hbm, hbm],
        out_specs=(vmem, free, free),
        scratch_shapes=[
            pltpu.VMEM((rows_dev, width), BF),
            pltpu.VMEM((rows_dev, width), BF),
            pltpu.VMEM((1, rows_dev), jnp.int32),
            pltpu.VMEM((width, ff), BF),
            pltpu.VMEM((ff, width), BF),
            pltpu.VMEM((group, 2 * width + 2 * LANES), BF),
            pltpu.VMEM((4 * group, 2 * width + 2 * LANES), BF),
            pltpu.VMEM((4 * MAIN, 2 * width), BF),
            pltpu.VMEM((rows, 2 * ff), BF),
            pltpu.VMEM((rows, width), BF),
            pltpu.VMEM((3 * chunk, width), BF),
            pltpu.VMEM((width, ff), F32),
            pltpu.VMEM((ff, width), F32),
            pltpu.VMEM((group, width + LANES), BF),
            pltpu.VMEM((group, width + LANES), BF),
            dma((5,)),
            dma((n_expert - 1,)),
            dma((n_expert,)),
            dma((n_expert,)),
            dma((n_expert,)),
            dma((4 * n_expert,)),
            dma((9,)),
            dma((9,)),
            dma((n_expert - 1,)),
            dma((n_expert,)),
            dma((8,)),
        ],
        compiler_params=pltpu.CompilerParams(
            collective_id=0, has_side_effects=True, vmem_limit_bytes=40 * 1024 * 1024
        ),
        cost_estimate=pl.CostEstimate(
            flops=10 * rows * width * ff, bytes_accessed=12 * width * ff, transcendentals=rows * ff
        ),
    )(tokens, upstream, task_ids.reshape(1, -1), task_expert, first, second)
    grad_in, grad_out = pl.pallas_call(
        deliver_kernel,
        out_shape=grads,
        in_specs=[free, free],
        out_specs=(free, free),
        scratch_shapes=[dma((8,))],
        cost_estimate=pl.CostEstimate(flops=0, bytes_accessed=16 * width * ff, transcendentals=0),
    )(grad_in, grad_out)
    return (token_grad, grad_in[None], grad_out[None])


def general_body(tokens, upstream, task_ids, task_expert, w_in, w_out):
    n_expert = lax.axis_size("expert")
    rows_dev = tokens.shape[0]
    width = tokens.shape[1]
    experts = task_expert.shape[0]
    capacity = max(2, (9 * rows_dev // 8 + n_expert - 1) // n_expert)
    lanes = jnp.arange(experts, dtype=jnp.int32)
    task_hot = (task_ids == lanes[None, :]).astype(jnp.int32)
    target = jnp.sum(task_hot * task_expert[None, :], axis=1)
    dest_hot = (target[:, None] == lanes[None, :]).astype(jnp.int32)
    before = jnp.cumsum(dest_hot, axis=0) - dest_hot
    rank = jnp.sum(before * dest_hot, axis=1)
    slot = target * capacity + rank
    packer = (jnp.arange(experts * capacity, dtype=jnp.int32)[:, None] == slot[None, :]).astype(
        jnp.bfloat16
    )
    send_rows = (
        jnp.dot(packer, tokens, preferred_element_type=jnp.float32)
        .astype(jnp.bfloat16)
        .reshape(experts, capacity, width)
    )
    send_grads = (
        jnp.dot(packer, upstream, preferred_element_type=jnp.float32)
        .astype(jnp.bfloat16)
        .reshape(experts, capacity, width)
    )
    first = w_in[0]
    second = w_out[0]
    got_rows, got_grads = (
        lax.all_to_all(send_rows, "expert", split_axis=0, concat_axis=0, tiled=True),
        lax.all_to_all(send_grads, "expert", split_axis=0, concat_axis=0, tiled=True),
    )
    got_rows = got_rows.reshape(experts * capacity, width)
    got_grads = got_grads.reshape(experts * capacity, width)
    all_rows, all_grads = (
        lax.all_gather(got_rows, "dp", axis=0, tiled=True),
        lax.all_gather(got_grads, "dp", axis=0, tiled=True),
    )
    pre = jnp.dot(all_rows, first, preferred_element_type=jnp.float32)
    act, slope = gelu_pair(pre)
    act = act.astype(jnp.bfloat16)
    grad_second = lax.dot_general(
        act, all_grads, (((0,), (0,)), ((), ())), preferred_element_type=jnp.float32
    )
    dact = lax.dot_general(
        all_grads, second, (((1,), (1,)), ((), ())), preferred_element_type=jnp.float32
    )
    dpre = (dact * slope).astype(jnp.bfloat16)
    grad_first = lax.dot_general(
        all_rows, dpre, (((0,), (0,)), ((), ())), preferred_element_type=jnp.float32
    )
    partial_value = lax.dot_general(
        dpre, first, (((1,), (1,)), ((), ())), preferred_element_type=jnp.float32
    )
    own = lax.psum_scatter(
        partial_value.astype(jnp.bfloat16), "dp", scatter_dimension=0, tiled=True
    ).astype(jnp.float32)
    own = own.astype(jnp.bfloat16).reshape(experts, capacity, width)
    back = lax.all_to_all(own, "expert", split_axis=0, concat_axis=0, tiled=True).reshape(
        experts * capacity, width
    )
    token_grad = lax.dot_general(
        packer, back, (((0,), (0,)), ((), ())), preferred_element_type=jnp.float32
    ).astype(jnp.bfloat16)
    return (token_grad, grad_first[None], grad_second[None])


def body(mesh, tokens, upstream, task_ids, task_expert, w_in, w_out):
    n_expert = mesh.shape["expert"]
    rows_dev, width = tokens.shape
    ff = w_in.shape[2]
    capacity = max(2, (9 * rows_dev // 8 + n_expert - 1) // n_expert)
    fits = (
        mesh.shape["dp"] == 4
        and n_expert == 8
        and rows_dev == 128
        and capacity <= MAIN + 2
        and width == n_expert * LANES
        and ff == width
    )
    run = fused_body if fits else general_body
    return run(tokens, upstream, task_ids, task_expert, w_in, w_out)


def solution(mesh):
    placed = (
        P(("dp", "expert"), None),
        P(("dp", "expert"), None),
        P(("dp", "expert"), None),
        P(),
        P("expert", None, "dp"),
        P("expert", "dp", None),
    )
    return jax.shard_map(
        functools.partial(body, mesh),
        mesh=mesh,
        in_specs=placed,
        out_specs=(P(("dp", "expert"), None), P("expert", None, "dp"), P("expert", "dp", None)),
        check_vma=False,
    )
```

```python
import functools

import jax
import jax.numpy as jnp
from jax import lax
from jax.experimental import pallas as pl
from jax.experimental.pallas import tpu as pltpu
from jax.sharding import PartitionSpec as P

coeff = 0.7978845608028654
MESH = pl.DeviceIdType.MESH
BF = jnp.bfloat16
F32 = jnp.float32
MAIN = 16
LANES = 128


def gelu_pair(pre):
    square = pre * pre
    tanh_val = jnp.tanh(pre * (coeff + coeff * 0.044715 * square))
    half = 0.5 + 0.5 * tanh_val
    slope = half + half * (1.0 - tanh_val) * (pre * (coeff + 3.0 * 0.044715 * coeff * square))
    return (pre * half, slope)


def fold(rows, width):
    return jnp.concatenate([rows[:, c : c + LANES] for c in range(0, width, LANES)], axis=0)


def unfold(rows, start, width):
    return jnp.concatenate(
        [rows[c * MAIN : (c + 1) * MAIN, start : start + LANES] for c in range(width // LANES)], axis=1
    )


def exchange_kernel(
    n_expert,
    rows_dev,
    width,
    ff,
    tokens_hbm,
    upstream_hbm,
    ids_hbm,
    experts_hbm,
    first_hbm,
    second_hbm,
    out_ref,
    grad_in_out,
    grad_out_out,
    tokens_ref,
    upstream_ref,
    ids_ref,
    experts_ref,
    first,
    second,
    send,
    got,
    extra,
    ad,
    part,
    peer,
    grad_in,
    grad_out,
    back_send,
    back_got,
    w_sem,
    z_send,
    x_send,
    y_send,
    f_send,
    recv,
    p_send,
    p_recv,
    b_send,
    b_recv,
    o_sem,
):
    chips = n_expert // 2
    group = n_expert * MAIN
    over = MAIN
    half = group // 2
    mains = 4 * group
    e = lax.axis_index("expert")
    d = lax.axis_index("dp")
    chip, core = lax.div(e, 2), lax.rem(e, 2)
    xn = d + 1 - 2 * lax.rem(d, 2)
    yn = lax.rem(d + 2, 4)
    diag = lax.rem(xn + 2, 4)
    upper = lax.div(chip, chips // 2)
    inner = chip + upper * (chips - 1 - 2 * chip)

    def order(i):
        place = (inner, 1 - inner, 2, 3)[i // 2]
        return (place + upper * (chips - 1 - 2 * place)) * 2 + lax.rem(core + i % 2, 2)

    def block(index):
        return pl.ds(pl.multiple_of(index * MAIN, MAIN), MAIN)

    def at(k, s):
        return pl.ds(pl.multiple_of(k * group + s * MAIN, MAIN), MAIN)

    loads = [
        pltpu.make_async_copy(src, dst, w_sem.at[i])
        for i, (src, dst) in enumerate(
            (
                (ids_hbm, ids_ref),
                (experts_hbm, experts_ref),
                (tokens_hbm, tokens_ref),
                (upstream_hbm, upstream_ref),
                (first_hbm, first),
                (second_hbm, second),
            )
        )
    ]
    for load in loads:
        load.start()

    barrier = pltpu.get_barrier_semaphore()
    for i in range(1, n_expert):
        pl.semaphore_signal(barrier, inc=1, device_id={"expert": order(i)}, device_id_type=MESH)
    for near in (xn, yn, diag):
        pl.semaphore_signal(barrier, inc=1, device_id={"dp": near}, device_id_type=MESH)

    row = lax.broadcasted_iota(jnp.int32, (rows_dev, rows_dev), 0)
    col = lax.broadcasted_iota(jnp.int32, (rows_dev, rows_dev), 1)
    line = row.astype(F32)
    earlier = (row < col).astype(BF)
    turned = (row >> 1 & 7) * 16 + (row >> 4) * 2 + (row & 1)
    perm = (turned == col).astype(BF)
    loads[0].wait()
    loads[1].wait()
    ids = ids_ref[...]
    goal = jnp.zeros(ids.shape, F32)
    for k in range(n_expert):
        goal = jnp.where(ids == k, experts_ref[k].astype(F32), goal)
    dest = (goal == line).astype(F32)
    before = jnp.dot(dest.astype(BF), earlier, preferred_element_type=F32)
    rank = jnp.sum(before * dest, axis=0, keepdims=True)
    is_main = (rank < MAIN).astype(F32)
    main_hot = ((goal * MAIN + rank == line).astype(F32) * is_main).astype(BF)
    over_hot = ((goal * 2 + (rank - MAIN) == line).astype(F32) * (1.0 - is_main)).astype(BF)[:over]

    def pick(hot_rows, values):
        return jnp.dot(hot_rows, values, preferred_element_type=F32).astype(BF)

    loads[2].wait()
    tokens = tokens_ref[...]
    send[:, :width] = pick(main_hot, tokens)
    loads[3].wait()
    upstream = upstream_ref[...]
    send[:, width : 2 * width] = pick(main_hot, upstream)
    folded = jnp.concatenate(
        [fold(pick(over_hot, tokens), width), fold(pick(over_hot, upstream), width)], axis=1
    )
    send[:, 2 * width :] = pick(perm, folded)

    pl.semaphore_wait(barrier, n_expert - 1 + 3)

    started = []

    def push(src, dst, send_sem, recv_sem, device):
        copy = pltpu.make_async_remote_copy(
            src_ref=src,
            dst_ref=dst,
            send_sem=send_sem,
            recv_sem=recv_sem,
            device_id=device,
            device_id_type=MESH,
        )
        copy.start()
        started.append(copy)

    def landed(here, sem):
        pltpu.make_async_copy(here, here, sem).wait()

    for i in range(1, n_expert):
        t = order(i)
        push(send.at[block(t)], got.at[at(0, e)], z_send.at[i - 1], recv.at[e], {"expert": t})
    got[at(0, e), :] = send[block(e), :]

    def arrived(k, s):
        landed(got.at[at(k, s)], recv.at[k * n_expert + s])

    def forward(i):
        s = order(i)
        arrived(1, s)
        arrived(2, s)
        if i % 2 == 0:
            push(got.at[at(1, s)], got.at[at(3, s)], f_send.at[i], recv.at[3 * n_expert + s], {"dp": yn})
        else:
            push(got.at[at(2, s)], got.at[at(3, s)], f_send.at[i], recv.at[3 * n_expert + s], {"dp": xn})

    lag = 2
    for i in range(n_expert):
        s = order(i)
        if i > 0:
            arrived(0, s)
        push(got.at[at(0, s)], got.at[at(1, s)], x_send.at[i], recv.at[n_expert + s], {"dp": xn})
        push(got.at[at(0, s)], got.at[at(2, s)], y_send.at[i], recv.at[2 * n_expert + s], {"dp": yn})
        if i >= lag:
            forward(i - lag)
    for i in range(n_expert - lag, n_expert):
        forward(i)
    for load in loads[4:]:
        load.wait()

    tile = 256

    def work(k, n):
        main = pl.ds(k * group, n * group)
        rest = pl.ds(k * over, n * over)
        tail = pl.ds(mains + k * over, n * over)
        cut = n * group
        for c in range(k, k + n):
            opened = pick(perm, got[pl.ds(c * group, group), 2 * width :])
            extra[pl.ds(c * over, over), :width] = unfold(opened, 0, width)
            extra[pl.ds(c * over, over), width:] = unfold(opened, LANES, width)

        @pl.loop(0, ff // tile)
        def _(f):
            cols = pl.ds(pl.multiple_of(f * tile, tile), tile)
            later = pl.ds(pl.multiple_of(ff + f * tile, tile), tile)
            rows = jnp.concatenate([got[main, :width], extra[rest, :width]], axis=0)
            grads = jnp.concatenate([got[main, width : 2 * width], extra[rest, width:]], axis=0)
            pre = jnp.dot(rows, first[:, cols], preferred_element_type=F32)
            act, slope = gelu_pair(pre)
            act = act.astype(BF)
            ad[main, cols] = act[:cut]
            ad[tail, cols] = act[cut:]
            dact = lax.dot_general(
                grads, second[cols, :], (((1,), (1,)), ((), ())), preferred_element_type=F32
            )
            dpre = (dact * slope).astype(BF)
            ad[main, later] = dpre[:cut]
            ad[tail, later] = dpre[cut:]

        @pl.loop(0, width // tile)
        def _(f):
            cols = pl.ds(pl.multiple_of(f * tile, tile), tile)
            dpre = jnp.concatenate([ad[main, ff:], ad[tail, ff:]], axis=0)
            value = lax.dot_general(
                dpre, first[cols, :], (((1,), (1,)), ((), ())), preferred_element_type=F32
            ).astype(BF)
            part[main, cols] = value[:cut]
            part[tail, cols] = value[cut:]

    far = (1 - upper) * half
    near = upper * half

    def spans(k):
        return (
            pl.ds(pl.multiple_of(k * group + far, half), half),
            pl.ds(mains + k * over, over),
            pl.ds(pl.multiple_of(k * group + near, half), half),
        )

    def slots(k):
        base = (k - 1) * group
        return (
            pl.ds(pl.multiple_of(base + far, half), half),
            pl.ds(3 * group + (k - 1) * over, over),
            pl.ds(pl.multiple_of(base + near, half), half),
        )

    def give(k, device):
        for j, (src, dst) in enumerate(zip(spans(k), slots(k))):
            i = 3 * (k - 1) + j
            push(part.at[src], peer.at[dst], p_send.at[i], p_recv.at[i], {"dp": device})

    work(1, 2)
    give(1, xn)
    give(2, yn)
    for i in range(n_expert):
        arrived(3, order(i))
    work(3, 1)
    give(3, diag)
    work(0, 1)

    def weight_grad(left, left_at, right, right_at, grad, grad_hbm, sems):
        @pl.loop(0, width // tile)
        def _(f):
            cols = pl.ds(pl.multiple_of(left_at + f * tile, tile), tile)
            mine = pl.ds(pl.multiple_of(f * tile, tile), tile)
            tall = jnp.concatenate([left[0][pl.ds(0, mains), cols], left[1][left[2], cols]], axis=0)
            wide = jnp.concatenate(
                [
                    right[0][pl.ds(0, mains), right_at : right_at + width],
                    right[1][right[2], right_at : right_at + width],
                ],
                axis=0,
            )
            grad[mine, :] = lax.dot_general(
                tall, wide, (((0,), (0,)), ((), ())), preferred_element_type=F32
            )
            pltpu.make_async_copy(grad.at[mine], grad_hbm.at[mine], o_sem.at[sems + f]).start()

    rows_all = (got, extra, pl.ds(0, 4 * over))
    hidden_all = (ad, ad, pl.ds(mains, 4 * over))
    weight_grad(hidden_all, 0, rows_all, width, grad_out, grad_out_out, 0)

    def total(j):
        value = part[spans(0)[j], :].astype(F32)
        for k in range(1, 4):
            landed(peer.at[slots(k)[j]], p_recv.at[3 * (k - 1) + j])
            value = value + peer[slots(k)[j], :].astype(F32)
        return value.astype(BF)

    def give_back(i):
        t = order(i)
        push(back_send.at[block(t)], back_got.at[block(e)], b_send.at[i - 1], b_recv.at[e], {"expert": t})

    back_send[pl.ds(pl.multiple_of(far, half), half), :width] = total(0)
    back_send[:, width:] = pick(perm, fold(total(1), width))
    for i in range(n_expert // 2, n_expert):
        give_back(i)
    back_send[pl.ds(pl.multiple_of(near, half), half), :width] = total(2)
    for i in range(1, n_expert // 2):
        give_back(i)
    back_got[block(e), :] = back_send[block(e), :]

    weight_grad(rows_all, 0, hidden_all, ff, grad_in, grad_in_out, 4)

    for i in range(1, n_expert):
        s = order(i)
        landed(back_got.at[block(s)], b_recv.at[s])
    extra_rows = unfold(pick(perm, back_got[:, width:]), 0, width)
    spec = (((0,), (0,)), ((), ()))
    result = lax.dot_general(main_hot, back_got[:, :width], spec, preferred_element_type=F32)
    result = result + lax.dot_general(over_hot, extra_rows, spec, preferred_element_type=F32)
    out_ref[...] = result.astype(BF)
    for copy in started:
        copy.wait_send()
    for f in range(width // tile):
        mine = pl.ds(f * tile, tile)
        pltpu.make_async_copy(grad_out.at[mine], grad_out_out.at[mine], o_sem.at[f]).wait()
        pltpu.make_async_copy(grad_in.at[mine], grad_in_out.at[mine], o_sem.at[4 + f]).wait()


def deliver_kernel(small, first, second, small_out, first_out, second_out, sem):
    rows = first.shape[0] // 4
    copies = [pltpu.make_async_copy(small, small_out, sem.at[8])]
    for i in range(4):
        here = pl.ds(i * rows, rows)
        copies.append(pltpu.make_async_copy(first.at[here], first_out.at[here], sem.at[2 * i]))
        copies.append(pltpu.make_async_copy(second.at[here], second_out.at[here], sem.at[2 * i + 1]))
    for copy in copies:
        copy.start()
    for copy in copies:
        copy.wait()


def fused_body(tokens, upstream, task_ids, task_expert, w_in, w_out):
    n_expert = lax.axis_size("expert")
    rows_dev, width = tokens.shape
    ff = w_in.shape[2]
    group = n_expert * MAIN
    chunk = group + MAIN
    rows = 4 * chunk
    first, second = w_in[0], w_out[0]
    dma = pltpu.SemaphoreType.DMA
    vmem = pl.BlockSpec(memory_space=pltpu.VMEM)
    hbm = pl.BlockSpec(memory_space=pltpu.HBM)
    free = pl.BlockSpec(memory_space=pl.ANY)
    results = (
        jax.ShapeDtypeStruct((rows_dev, width), BF),
        jax.ShapeDtypeStruct((width, ff), F32),
        jax.ShapeDtypeStruct((ff, width), F32),
    )
    held = (tokens, upstream, task_ids.reshape(1, -1), task_expert, first, second)
    token_grad, grad_in, grad_out = pl.pallas_call(
        functools.partial(exchange_kernel, n_expert, rows_dev, width, ff),
        out_shape=results,
        in_specs=[hbm] * 6,
        out_specs=(vmem, free, free),
        scratch_shapes=[
            pltpu.VMEM((rows_dev, width), BF),
            pltpu.VMEM((rows_dev, width), BF),
            pltpu.VMEM((1, rows_dev), jnp.int32),
            pltpu.SMEM(task_expert.shape, jnp.int32),
            pltpu.VMEM((width, ff), BF),
            pltpu.VMEM((ff, width), BF),
            pltpu.VMEM((group, 2 * width + 2 * LANES), BF),
            pltpu.VMEM((4 * group, 2 * width + 2 * LANES), BF),
            pltpu.VMEM((4 * MAIN, 2 * width), BF),
            pltpu.VMEM((rows, 2 * ff), BF),
            pltpu.VMEM((rows, width), BF),
            pltpu.VMEM((3 * chunk, width), BF),
            pltpu.VMEM((width, ff), F32),
            pltpu.VMEM((ff, width), F32),
            pltpu.VMEM((group, width + LANES), BF),
            pltpu.VMEM((group, width + LANES), BF),
            dma((6,)),
            dma((n_expert - 1,)),
            dma((n_expert,)),
            dma((n_expert,)),
            dma((n_expert,)),
            dma((4 * n_expert,)),
            dma((9,)),
            dma((9,)),
            dma((n_expert - 1,)),
            dma((n_expert,)),
            dma((8,)),
        ],
        compiler_params=pltpu.CompilerParams(
            collective_id=0, has_side_effects=True, vmem_limit_bytes=40 * 1024 * 1024
        ),
        cost_estimate=pl.CostEstimate(
            flops=10 * rows * width * ff, bytes_accessed=12 * width * ff, transcendentals=rows * ff
        ),
    )(*(pltpu.with_memory_space_constraint(x, pltpu.HBM) for x in held))
    token_grad, grad_in, grad_out = pl.pallas_call(
        deliver_kernel,
        out_shape=results,
        in_specs=[free, free, free],
        out_specs=(free, free, free),
        scratch_shapes=[dma((9,))],
        compiler_params=pltpu.CompilerParams(vmem_limit_bytes=1024 * 1024),
        cost_estimate=pl.CostEstimate(flops=0, bytes_accessed=16 * width * ff, transcendentals=0),
    )(token_grad, grad_in, grad_out)
    return (token_grad, grad_in[None], grad_out[None])


def general_body(tokens, upstream, task_ids, task_expert, w_in, w_out):
    n_expert = lax.axis_size("expert")
    rows_dev = tokens.shape[0]
    width = tokens.shape[1]
    experts = task_expert.shape[0]
    capacity = max(2, (9 * rows_dev // 8 + n_expert - 1) // n_expert)
    lanes = jnp.arange(experts, dtype=jnp.int32)
    task_hot = (task_ids == lanes[None, :]).astype(jnp.int32)
    target = jnp.sum(task_hot * task_expert[None, :], axis=1)
    dest_hot = (target[:, None] == lanes[None, :]).astype(jnp.int32)
    before = jnp.cumsum(dest_hot, axis=0) - dest_hot
    rank = jnp.sum(before * dest_hot, axis=1)
    slot = target * capacity + rank
    packer = (jnp.arange(experts * capacity, dtype=jnp.int32)[:, None] == slot[None, :]).astype(
        jnp.bfloat16
    )
    send_rows = (
        jnp.dot(packer, tokens, preferred_element_type=jnp.float32)
        .astype(jnp.bfloat16)
        .reshape(experts, capacity, width)
    )
    send_grads = (
        jnp.dot(packer, upstream, preferred_element_type=jnp.float32)
        .astype(jnp.bfloat16)
        .reshape(experts, capacity, width)
    )
    first = w_in[0]
    second = w_out[0]
    got_rows, got_grads = (
        lax.all_to_all(send_rows, "expert", split_axis=0, concat_axis=0, tiled=True),
        lax.all_to_all(send_grads, "expert", split_axis=0, concat_axis=0, tiled=True),
    )
    got_rows = got_rows.reshape(experts * capacity, width)
    got_grads = got_grads.reshape(experts * capacity, width)
    all_rows, all_grads = (
        lax.all_gather(got_rows, "dp", axis=0, tiled=True),
        lax.all_gather(got_grads, "dp", axis=0, tiled=True),
    )
    pre = jnp.dot(all_rows, first, preferred_element_type=jnp.float32)
    act, slope = gelu_pair(pre)
    act = act.astype(jnp.bfloat16)
    grad_second = lax.dot_general(
        act, all_grads, (((0,), (0,)), ((), ())), preferred_element_type=jnp.float32
    )
    dact = lax.dot_general(
        all_grads, second, (((1,), (1,)), ((), ())), preferred_element_type=jnp.float32
    )
    dpre = (dact * slope).astype(jnp.bfloat16)
    grad_first = lax.dot_general(
        all_rows, dpre, (((0,), (0,)), ((), ())), preferred_element_type=jnp.float32
    )
    partial_value = lax.dot_general(
        dpre, first, (((1,), (1,)), ((), ())), preferred_element_type=jnp.float32
    )
    own = lax.psum_scatter(
        partial_value.astype(jnp.bfloat16), "dp", scatter_dimension=0, tiled=True
    ).astype(jnp.float32)
    own = own.astype(jnp.bfloat16).reshape(experts, capacity, width)
    back = lax.all_to_all(own, "expert", split_axis=0, concat_axis=0, tiled=True).reshape(
        experts * capacity, width
    )
    token_grad = lax.dot_general(
        packer, back, (((0,), (0,)), ((), ())), preferred_element_type=jnp.float32
    ).astype(jnp.bfloat16)
    return (token_grad, grad_first[None], grad_second[None])


def body(mesh, tokens, upstream, task_ids, task_expert, w_in, w_out):
    n_expert = mesh.shape["expert"]
    rows_dev, width = tokens.shape
    ff = w_in.shape[2]
    capacity = max(2, (9 * rows_dev // 8 + n_expert - 1) // n_expert)
    fits = (
        mesh.shape["dp"] == 4
        and n_expert == 8
        and rows_dev == 128
        and capacity <= MAIN + 2
        and width == n_expert * LANES
        and ff == width
    )
    run = fused_body if fits else general_body
    return run(tokens, upstream, task_ids, task_expert, w_in, w_out)


def solution(mesh):
    placed = (
        P(("dp", "expert"), None),
        P(("dp", "expert"), None),
        P(("dp", "expert"), None),
        P(),
        P("expert", None, "dp"),
        P("expert", "dp", None),
    )
    return jax.shard_map(
        functools.partial(body, mesh),
        mesh=mesh,
        in_specs=placed,
        out_specs=(P(("dp", "expert"), None), P("expert", None, "dp"), P("expert", "dp", None)),
        check_vma=False,
    )
```

```python
import functools

import jax
import jax.numpy as jnp
from jax import lax
from jax.experimental import pallas as pl
from jax.experimental.pallas import tpu as pltpu
from jax.sharding import PartitionSpec as P

coeff = 0.7978845608028654
MESH = pl.DeviceIdType.MESH
BF = jnp.bfloat16
F32 = jnp.float32
MAIN = 16
LANES = 128


def gelu_pair(pre):
    square = pre * pre
    tanh_val = jnp.tanh(pre * (coeff + coeff * 0.044715 * square))
    half = 0.5 + 0.5 * tanh_val
    slope = half + half * (1.0 - tanh_val) * (pre * (coeff + 3.0 * 0.044715 * coeff * square))
    return (pre * half, slope)


def fold(rows, width):
    return jnp.concatenate([rows[:, c : c + LANES] for c in range(0, width, LANES)], axis=0)


def unfold(rows, start, width):
    return jnp.concatenate(
        [rows[c * MAIN : (c + 1) * MAIN, start : start + LANES] for c in range(width // LANES)], axis=1
    )


def exchange_kernel(
    n_expert,
    rows_dev,
    width,
    ff,
    tokens_hbm,
    upstream_hbm,
    ids_hbm,
    experts_hbm,
    first_hbm,
    second_hbm,
    out_ref,
    grad_in_out,
    grad_out_out,
    tokens_ref,
    upstream_ref,
    ids_ref,
    experts_ref,
    first,
    second,
    send,
    got,
    extra,
    ad,
    part,
    middle,
    peer_x,
    peer_y,
    grad_in,
    grad_out,
    back_send,
    back_got,
    w_sem,
    z_send,
    x_send,
    y_send,
    f_send,
    recv,
    p_send,
    p_recv,
    b_send,
    b_recv,
    o_sem,
):
    chips = n_expert // 2
    group = n_expert * MAIN
    over = MAIN
    half = group // 2
    chunk = group + over
    mains = 4 * group
    e = lax.axis_index("expert")
    d = lax.axis_index("dp")
    chip, core = lax.div(e, 2), lax.rem(e, 2)
    xn = d + 1 - 2 * lax.rem(d, 2)
    yn = lax.rem(d + 2, 4)
    diag = lax.rem(xn + 2, 4)
    upper = lax.div(chip, chips // 2)
    inner = chip + upper * (chips - 1 - 2 * chip)

    def order(i):
        place = (inner, 1 - inner, 2, 3)[i // 2]
        return (place + upper * (chips - 1 - 2 * place)) * 2 + lax.rem(core + i % 2, 2)

    def block(index):
        return pl.ds(pl.multiple_of(index * MAIN, MAIN), MAIN)

    def at(k, s):
        return pl.ds(pl.multiple_of(k * group + s * MAIN, MAIN), MAIN)

    loads = [
        pltpu.make_async_copy(src, dst, w_sem.at[i])
        for i, (src, dst) in enumerate(
            (
                (ids_hbm, ids_ref),
                (experts_hbm, experts_ref),
                (tokens_hbm, tokens_ref),
                (upstream_hbm, upstream_ref),
                (first_hbm, first),
                (second_hbm, second),
            )
        )
    ]
    for load in loads:
        load.start()

    barrier = pltpu.get_barrier_semaphore()
    for i in range(1, n_expert):
        pl.semaphore_signal(barrier, inc=1, device_id={"expert": order(i)}, device_id_type=MESH)
    for near in (xn, yn, diag):
        pl.semaphore_signal(barrier, inc=1, device_id={"dp": near}, device_id_type=MESH)

    row = lax.broadcasted_iota(jnp.int32, (rows_dev, rows_dev), 0)
    col = lax.broadcasted_iota(jnp.int32, (rows_dev, rows_dev), 1)
    line = row.astype(F32)
    earlier = (row < col).astype(BF)
    turned = (row >> 1 & 7) * 16 + (row >> 4) * 2 + (row & 1)
    perm = (turned == col).astype(BF)
    loads[0].wait()
    loads[1].wait()
    ids = ids_ref[...]
    goal = jnp.zeros(ids.shape, F32)
    for k in range(n_expert):
        goal = jnp.where(ids == k, experts_ref[k].astype(F32), goal)
    dest = (goal == line).astype(F32)
    before = jnp.dot(dest.astype(BF), earlier, preferred_element_type=F32)
    rank = jnp.sum(before * dest, axis=0, keepdims=True)
    is_main = (rank < MAIN).astype(F32)
    main_hot = ((goal * MAIN + rank == line).astype(F32) * is_main).astype(BF)
    over_hot = ((goal * 2 + (rank - MAIN) == line).astype(F32) * (1.0 - is_main)).astype(BF)[:over]

    def pick(hot_rows, values):
        return jnp.dot(hot_rows, values, preferred_element_type=F32).astype(BF)

    loads[2].wait()
    tokens = tokens_ref[...]
    send[:, :width] = pick(main_hot, tokens)
    loads[3].wait()
    upstream = upstream_ref[...]
    send[:, width : 2 * width] = pick(main_hot, upstream)
    folded = jnp.concatenate(
        [fold(pick(over_hot, tokens), width), fold(pick(over_hot, upstream), width)], axis=1
    )
    send[:, 2 * width :] = pick(perm, folded)

    pl.semaphore_wait(barrier, n_expert - 1 + 3)

    started = []

    def push(src, dst, send_sem, recv_sem, device):
        copy = pltpu.make_async_remote_copy(
            src_ref=src,
            dst_ref=dst,
            send_sem=send_sem,
            recv_sem=recv_sem,
            device_id=device,
            device_id_type=MESH,
        )
        copy.start()
        started.append(copy)

    def landed(here, sem):
        pltpu.make_async_copy(here, here, sem).wait()

    for i in range(1, n_expert):
        t = order(i)
        push(send.at[block(t)], got.at[at(0, e)], z_send.at[i - 1], recv.at[e], {"expert": t})
    got[at(0, e), :] = send[block(e), :]

    def arrived(k, s):
        landed(got.at[at(k, s)], recv.at[k * n_expert + s])

    def forward(i):
        s = order(i)
        arrived(1, s)
        arrived(2, s)
        if i % 2 == 0:
            push(got.at[at(1, s)], got.at[at(3, s)], f_send.at[i], recv.at[3 * n_expert + s], {"dp": yn})
        else:
            push(got.at[at(2, s)], got.at[at(3, s)], f_send.at[i], recv.at[3 * n_expert + s], {"dp": xn})

    lag = 2
    for i in range(n_expert):
        s = order(i)
        if i > 0:
            arrived(0, s)
        push(got.at[at(0, s)], got.at[at(1, s)], x_send.at[i], recv.at[n_expert + s], {"dp": xn})
        push(got.at[at(0, s)], got.at[at(2, s)], y_send.at[i], recv.at[2 * n_expert + s], {"dp": yn})
        if i >= lag:
            forward(i - lag)
    for i in range(n_expert - lag, n_expert):
        forward(i)
    for load in loads[4:]:
        load.wait()

    tile = 256

    def work(k, n):
        main = pl.ds(k * group, n * group)
        rest = pl.ds(k * over, n * over)
        tail = pl.ds(mains + k * over, n * over)
        cut = n * group
        for c in range(k, k + n):
            opened = pick(perm, got[pl.ds(c * group, group), 2 * width :])
            extra[pl.ds(c * over, over), :width] = unfold(opened, 0, width)
            extra[pl.ds(c * over, over), width:] = unfold(opened, LANES, width)

        @pl.loop(0, ff // tile)
        def _(f):
            cols = pl.ds(pl.multiple_of(f * tile, tile), tile)
            later = pl.ds(pl.multiple_of(ff + f * tile, tile), tile)
            rows = jnp.concatenate([got[main, :width], extra[rest, :width]], axis=0)
            grads = jnp.concatenate([got[main, width : 2 * width], extra[rest, width:]], axis=0)
            pre = jnp.dot(rows, first[:, cols], preferred_element_type=F32)
            act, slope = gelu_pair(pre)
            act = act.astype(BF)
            ad[main, cols] = act[:cut]
            ad[tail, cols] = act[cut:]
            dact = lax.dot_general(
                grads, second[cols, :], (((1,), (1,)), ((), ())), preferred_element_type=F32
            )
            dpre = (dact * slope).astype(BF)
            ad[main, later] = dpre[:cut]
            ad[tail, later] = dpre[cut:]

        @pl.loop(0, width // tile)
        def _(f):
            cols = pl.ds(pl.multiple_of(f * tile, tile), tile)
            dpre = jnp.concatenate([ad[main, ff:], ad[tail, ff:]], axis=0)
            value = lax.dot_general(
                dpre, first[cols, :], (((1,), (1,)), ((), ())), preferred_element_type=F32
            ).astype(BF)
            for c in range(n):
                base = (k + c) * chunk
                low = pl.multiple_of(base + (1 - upper) * (half + over), over)
                high = pl.multiple_of(base + upper * (half + over), over)
                part[pl.ds(low, half), cols] = value[c * group : c * group + half]
                part[pl.ds(high, half), cols] = value[c * group + half : (c + 1) * group]
                part[pl.ds(base + half, over), cols] = value[cut + c * over : cut + (c + 1) * over]

    far = (1 - upper) * half
    near = upper * half
    spans = ((0, half + over), (half + over, half))
    left, right = pl.ds(0, width // 2), pl.ds(width // 2, width // 2)

    def give(k, low, size, cols, dst, i, device):
        push(
            part.at[pl.ds(k * chunk + low, size), cols],
            dst.at[pl.ds(low, size), cols],
            p_send.at[i],
            p_recv.at[i],
            {"dp": device},
        )

    work(1, 2)
    give(1, 0, chunk, left, peer_x, 0, xn)
    give(2, 0, chunk, right, peer_y, 1, yn)
    for i in range(n_expert):
        arrived(3, order(i))
    work(3, 1)
    for j, (low, size) in enumerate(spans):
        give(3, low, size, left, middle, 2 + 2 * j, xn)
        give(3, low, size, right, middle, 3 + 2 * j, yn)
    work(0, 1)
    for j, (low, size) in enumerate(spans):
        here = pl.ds(low, size)
        for k, cols, dst, near_dev, m in ((2, left, peer_y, yn, 0), (1, right, peer_x, xn, 1)):
            mine = pl.ds(k * chunk + low, size)
            landed(middle.at[here, cols], p_recv.at[2 + 2 * j + m])
            value = part[mine, cols].astype(F32) + middle[here, cols].astype(F32)
            part[mine, cols] = value.astype(BF)
            give(k, low, size, cols, dst, 6 + 2 * j + m, near_dev)

    def weight_grad(left, left_at, right, right_at, grad, grad_hbm, sems):
        @pl.loop(0, width // tile)
        def _(f):
            cols = pl.ds(pl.multiple_of(left_at + f * tile, tile), tile)
            mine = pl.ds(pl.multiple_of(f * tile, tile), tile)
            tall = jnp.concatenate([left[0][pl.ds(0, mains), cols], left[1][left[2], cols]], axis=0)
            wide = jnp.concatenate(
                [
                    right[0][pl.ds(0, mains), right_at : right_at + width],
                    right[1][right[2], right_at : right_at + width],
                ],
                axis=0,
            )
            grad[mine, :] = lax.dot_general(
                tall, wide, (((0,), (0,)), ((), ())), preferred_element_type=F32
            )
            pltpu.make_async_copy(grad.at[mine], grad_hbm.at[mine], o_sem.at[sems + f]).start()

    rows_all = (got, extra, pl.ds(0, 4 * over))
    hidden_all = (ad, ad, pl.ds(mains, 4 * over))
    weight_grad(hidden_all, 0, rows_all, width, grad_out, grad_out_out, 0)

    landed(peer_x.at[pl.ds(0, chunk), left], p_recv.at[0])
    landed(peer_y.at[pl.ds(0, chunk), right], p_recv.at[1])

    def total(j):
        low, size = spans[j]
        here = pl.ds(low, size)
        landed(peer_y.at[here, left], p_recv.at[6 + 2 * j])
        landed(peer_x.at[here, right], p_recv.at[7 + 2 * j])
        value = part[here, :].astype(F32) + peer_x[here, :].astype(F32) + peer_y[here, :].astype(F32)
        return value.astype(BF)

    def give_back(i):
        t = order(i)
        push(back_send.at[block(t)], back_got.at[block(e)], b_send.at[i - 1], b_recv.at[e], {"expert": t})

    first_rows = total(0)
    back_send[pl.ds(pl.multiple_of(far, half), half), :width] = first_rows[:half]
    back_send[:, width:] = pick(perm, fold(first_rows[half:], width))
    for i in range(n_expert // 2, n_expert):
        give_back(i)
    back_send[pl.ds(pl.multiple_of(near, half), half), :width] = total(1)
    for i in range(1, n_expert // 2):
        give_back(i)
    back_got[block(e), :] = back_send[block(e), :]

    weight_grad(rows_all, 0, hidden_all, ff, grad_in, grad_in_out, 4)

    for i in range(1, n_expert):
        s = order(i)
        landed(back_got.at[block(s)], b_recv.at[s])
    extra_rows = unfold(pick(perm, back_got[:, width:]), 0, width)
    spec = (((0,), (0,)), ((), ()))
    result = lax.dot_general(main_hot, back_got[:, :width], spec, preferred_element_type=F32)
    result = result + lax.dot_general(over_hot, extra_rows, spec, preferred_element_type=F32)
    out_ref[...] = result.astype(BF)
    for copy in started:
        copy.wait_send()
    for f in range(width // tile):
        mine = pl.ds(f * tile, tile)
        pltpu.make_async_copy(grad_out.at[mine], grad_out_out.at[mine], o_sem.at[f]).wait()
        pltpu.make_async_copy(grad_in.at[mine], grad_in_out.at[mine], o_sem.at[4 + f]).wait()


def deliver_kernel(small, first, second, small_out, first_out, second_out, sem):
    rows = first.shape[0] // 4
    copies = [pltpu.make_async_copy(small, small_out, sem.at[8])]
    for i in range(4):
        here = pl.ds(i * rows, rows)
        copies.append(pltpu.make_async_copy(first.at[here], first_out.at[here], sem.at[2 * i]))
        copies.append(pltpu.make_async_copy(second.at[here], second_out.at[here], sem.at[2 * i + 1]))
    for copy in copies:
        copy.start()
    for copy in copies:
        copy.wait()


def fused_body(tokens, upstream, task_ids, task_expert, w_in, w_out):
    n_expert = lax.axis_size("expert")
    rows_dev, width = tokens.shape
    ff = w_in.shape[2]
    group = n_expert * MAIN
    chunk = group + MAIN
    rows = 4 * chunk
    first, second = w_in[0], w_out[0]
    dma = pltpu.SemaphoreType.DMA
    vmem = pl.BlockSpec(memory_space=pltpu.VMEM)
    hbm = pl.BlockSpec(memory_space=pltpu.HBM)
    free = pl.BlockSpec(memory_space=pl.ANY)
    results = (
        jax.ShapeDtypeStruct((rows_dev, width), BF),
        jax.ShapeDtypeStruct((width, ff), F32),
        jax.ShapeDtypeStruct((ff, width), F32),
    )
    held = (tokens, upstream, task_ids.reshape(1, -1), task_expert, first, second)
    token_grad, grad_in, grad_out = pl.pallas_call(
        functools.partial(exchange_kernel, n_expert, rows_dev, width, ff),
        out_shape=results,
        in_specs=[hbm] * 6,
        out_specs=(vmem, free, free),
        scratch_shapes=[
            pltpu.VMEM((rows_dev, width), BF),
            pltpu.VMEM((rows_dev, width), BF),
            pltpu.VMEM((1, rows_dev), jnp.int32),
            pltpu.SMEM(task_expert.shape, jnp.int32),
            pltpu.VMEM((width, ff), BF),
            pltpu.VMEM((ff, width), BF),
            pltpu.VMEM((group, 2 * width + 2 * LANES), BF),
            pltpu.VMEM((4 * group, 2 * width + 2 * LANES), BF),
            pltpu.VMEM((4 * MAIN, 2 * width), BF),
            pltpu.VMEM((rows, 2 * ff), BF),
            pltpu.VMEM((rows, width), BF),
            pltpu.VMEM((chunk, width), BF),
            pltpu.VMEM((chunk, width), BF),
            pltpu.VMEM((chunk, width), BF),
            pltpu.VMEM((width, ff), F32),
            pltpu.VMEM((ff, width), F32),
            pltpu.VMEM((group, width + LANES), BF),
            pltpu.VMEM((group, width + LANES), BF),
            dma((6,)),
            dma((n_expert - 1,)),
            dma((n_expert,)),
            dma((n_expert,)),
            dma((n_expert,)),
            dma((4 * n_expert,)),
            dma((10,)),
            dma((10,)),
            dma((n_expert - 1,)),
            dma((n_expert,)),
            dma((8,)),
        ],
        compiler_params=pltpu.CompilerParams(
            collective_id=0, has_side_effects=True, vmem_limit_bytes=40 * 1024 * 1024
        ),
        cost_estimate=pl.CostEstimate(
            flops=10 * rows * width * ff, bytes_accessed=12 * width * ff, transcendentals=rows * ff
        ),
    )(*(pltpu.with_memory_space_constraint(x, pltpu.HBM) for x in held))
    token_grad, grad_in, grad_out = pl.pallas_call(
        deliver_kernel,
        out_shape=results,
        in_specs=[free, free, free],
        out_specs=(free, free, free),
        scratch_shapes=[dma((9,))],
        compiler_params=pltpu.CompilerParams(vmem_limit_bytes=1024 * 1024),
        cost_estimate=pl.CostEstimate(flops=0, bytes_accessed=16 * width * ff, transcendentals=0),
    )(token_grad, grad_in, grad_out)
    return (token_grad, grad_in[None], grad_out[None])


def general_body(tokens, upstream, task_ids, task_expert, w_in, w_out):
    n_expert = lax.axis_size("expert")
    rows_dev = tokens.shape[0]
    width = tokens.shape[1]
    experts = task_expert.shape[0]
    capacity = max(2, (9 * rows_dev // 8 + n_expert - 1) // n_expert)
    lanes = jnp.arange(experts, dtype=jnp.int32)
    task_hot = (task_ids == lanes[None, :]).astype(jnp.int32)
    target = jnp.sum(task_hot * task_expert[None, :], axis=1)
    dest_hot = (target[:, None] == lanes[None, :]).astype(jnp.int32)
    before = jnp.cumsum(dest_hot, axis=0) - dest_hot
    rank = jnp.sum(before * dest_hot, axis=1)
    slot = target * capacity + rank
    packer = (jnp.arange(experts * capacity, dtype=jnp.int32)[:, None] == slot[None, :]).astype(
        jnp.bfloat16
    )
    send_rows = (
        jnp.dot(packer, tokens, preferred_element_type=jnp.float32)
        .astype(jnp.bfloat16)
        .reshape(experts, capacity, width)
    )
    send_grads = (
        jnp.dot(packer, upstream, preferred_element_type=jnp.float32)
        .astype(jnp.bfloat16)
        .reshape(experts, capacity, width)
    )
    first = w_in[0]
    second = w_out[0]
    got_rows, got_grads = (
        lax.all_to_all(send_rows, "expert", split_axis=0, concat_axis=0, tiled=True),
        lax.all_to_all(send_grads, "expert", split_axis=0, concat_axis=0, tiled=True),
    )
    got_rows = got_rows.reshape(experts * capacity, width)
    got_grads = got_grads.reshape(experts * capacity, width)
    all_rows, all_grads = (
        lax.all_gather(got_rows, "dp", axis=0, tiled=True),
        lax.all_gather(got_grads, "dp", axis=0, tiled=True),
    )
    pre = jnp.dot(all_rows, first, preferred_element_type=jnp.float32)
    act, slope = gelu_pair(pre)
    act = act.astype(jnp.bfloat16)
    grad_second = lax.dot_general(
        act, all_grads, (((0,), (0,)), ((), ())), preferred_element_type=jnp.float32
    )
    dact = lax.dot_general(
        all_grads, second, (((1,), (1,)), ((), ())), preferred_element_type=jnp.float32
    )
    dpre = (dact * slope).astype(jnp.bfloat16)
    grad_first = lax.dot_general(
        all_rows, dpre, (((0,), (0,)), ((), ())), preferred_element_type=jnp.float32
    )
    partial_value = lax.dot_general(
        dpre, first, (((1,), (1,)), ((), ())), preferred_element_type=jnp.float32
    )
    own = lax.psum_scatter(
        partial_value.astype(jnp.bfloat16), "dp", scatter_dimension=0, tiled=True
    ).astype(jnp.float32)
    own = own.astype(jnp.bfloat16).reshape(experts, capacity, width)
    back = lax.all_to_all(own, "expert", split_axis=0, concat_axis=0, tiled=True).reshape(
        experts * capacity, width
    )
    token_grad = lax.dot_general(
        packer, back, (((0,), (0,)), ((), ())), preferred_element_type=jnp.float32
    ).astype(jnp.bfloat16)
    return (token_grad, grad_first[None], grad_second[None])


def body(mesh, tokens, upstream, task_ids, task_expert, w_in, w_out):
    n_expert = mesh.shape["expert"]
    rows_dev, width = tokens.shape
    ff = w_in.shape[2]
    capacity = max(2, (9 * rows_dev // 8 + n_expert - 1) // n_expert)
    fits = (
        mesh.shape["dp"] == 4
        and n_expert == 8
        and rows_dev == 128
        and capacity <= MAIN + 2
        and width == n_expert * LANES
        and ff == width
    )
    run = fused_body if fits else general_body
    return run(tokens, upstream, task_ids, task_expert, w_in, w_out)


def solution(mesh):
    placed = (
        P(("dp", "expert"), None),
        P(("dp", "expert"), None),
        P(("dp", "expert"), None),
        P(),
        P("expert", None, "dp"),
        P("expert", "dp", None),
    )
    return jax.shard_map(
        functools.partial(body, mesh),
        mesh=mesh,
        in_specs=placed,
        out_specs=(P(("dp", "expert"), None), P("expert", None, "dp"), P("expert", "dp", None)),
        check_vma=False,
    )
```

```python
import functools

import jax
import jax.numpy as jnp
from jax import lax
from jax.experimental import pallas as pl
from jax.experimental.pallas import tpu as pltpu
from jax.sharding import PartitionSpec as P

coeff = 0.7978845608028654
MESH = pl.DeviceIdType.MESH
BF = jnp.bfloat16
F32 = jnp.float32
MAIN = 16
LANES = 128


def gelu_pair(pre):
    square = pre * pre
    tanh_val = jnp.tanh(pre * (coeff + coeff * 0.044715 * square))
    half = 0.5 + 0.5 * tanh_val
    slope = half + half * (1.0 - tanh_val) * (pre * (coeff + 3.0 * 0.044715 * coeff * square))
    return (pre * half, slope)


def fold(rows, width):
    return jnp.concatenate([rows[:, c : c + LANES] for c in range(0, width, LANES)], axis=0)


def unfold(rows, start, width):
    return jnp.concatenate(
        [rows[c * MAIN : (c + 1) * MAIN, start : start + LANES] for c in range(width // LANES)], axis=1
    )


def exchange_kernel(
    n_expert,
    rows_dev,
    width,
    ff,
    tokens_hbm,
    upstream_hbm,
    ids_hbm,
    experts_hbm,
    first_hbm,
    second_hbm,
    out_ref,
    grad_in_out,
    grad_out_out,
    tokens_ref,
    upstream_ref,
    ids_ref,
    experts_ref,
    first,
    second,
    send,
    got,
    extra,
    ad,
    part,
    middle,
    peer_x,
    peer_y,
    grad_in,
    grad_out,
    back_send,
    back_got,
    w_sem,
    z_send,
    x_send,
    y_send,
    f_send,
    recv,
    p_send,
    p_recv,
    b_send,
    b_recv,
    o_sem,
):
    chips = n_expert // 2
    group = n_expert * MAIN
    over = MAIN
    half = group // 2
    chunk = group + over
    mains = 4 * group
    e = lax.axis_index("expert")
    d = lax.axis_index("dp")
    chip, core = lax.div(e, 2), lax.rem(e, 2)
    xn = d + 1 - 2 * lax.rem(d, 2)
    yn = lax.rem(d + 2, 4)
    diag = lax.rem(xn + 2, 4)
    upper = lax.div(chip, chips // 2)
    inner = chip + upper * (chips - 1 - 2 * chip)

    def order(i):
        place = (inner, 1 - inner, 2, 3)[i // 2]
        return (place + upper * (chips - 1 - 2 * place)) * 2 + lax.rem(core + i % 2, 2)

    def block(index):
        return pl.ds(pl.multiple_of(index * MAIN, MAIN), MAIN)

    def at(k, s):
        return pl.ds(pl.multiple_of(k * group + s * MAIN, MAIN), MAIN)

    loads = [
        pltpu.make_async_copy(src, dst, w_sem.at[i])
        for i, (src, dst) in enumerate(
            (
                (ids_hbm, ids_ref),
                (experts_hbm, experts_ref),
                (tokens_hbm, tokens_ref),
                (upstream_hbm, upstream_ref),
                (first_hbm, first),
                (second_hbm, second),
            )
        )
    ]
    for load in loads:
        load.start()

    barrier = pltpu.get_barrier_semaphore()
    for i in range(1, n_expert):
        pl.semaphore_signal(barrier, inc=1, device_id={"expert": order(i)}, device_id_type=MESH)
    for near in (xn, yn, diag):
        pl.semaphore_signal(barrier, inc=1, device_id={"dp": near}, device_id_type=MESH)

    row = lax.broadcasted_iota(jnp.int32, (rows_dev, rows_dev), 0)
    col = lax.broadcasted_iota(jnp.int32, (rows_dev, rows_dev), 1)
    line = row.astype(F32)
    earlier = (row < col).astype(BF)
    turned = (row >> 1 & 7) * 16 + (row >> 4) * 2 + (row & 1)
    perm = (turned == col).astype(BF)
    loads[0].wait()
    loads[1].wait()
    ids = ids_ref[...]
    goal = jnp.zeros(ids.shape, F32)
    for k in range(n_expert):
        goal = jnp.where(ids == k, experts_ref[k].astype(F32), goal)
    dest = (goal == line).astype(F32)
    before = jnp.dot(dest.astype(BF), earlier, preferred_element_type=F32)
    rank = jnp.sum(before * dest, axis=0, keepdims=True)
    is_main = (rank < MAIN).astype(F32)
    main_hot = ((goal * MAIN + rank == line).astype(F32) * is_main).astype(BF)
    over_hot = ((goal * 2 + (rank - MAIN) == line).astype(F32) * (1.0 - is_main)).astype(BF)[:over]

    def pick(hot_rows, values):
        return jnp.dot(hot_rows, values, preferred_element_type=F32).astype(BF)

    loads[2].wait()
    tokens = tokens_ref[...]
    send[:, :width] = pick(main_hot, tokens)
    loads[3].wait()
    upstream = upstream_ref[...]
    send[:, width : 2 * width] = pick(main_hot, upstream)
    folded = jnp.concatenate(
        [fold(pick(over_hot, tokens), width), fold(pick(over_hot, upstream), width)], axis=1
    )
    send[:, 2 * width :] = pick(perm, folded)

    pl.semaphore_wait(barrier, n_expert - 1 + 3)

    started = []

    def push(src, dst, send_sem, recv_sem, device):
        copy = pltpu.make_async_remote_copy(
            src_ref=src,
            dst_ref=dst,
            send_sem=send_sem,
            recv_sem=recv_sem,
            device_id=device,
            device_id_type=MESH,
        )
        copy.start()
        started.append(copy)

    def landed(here, sem):
        pltpu.make_async_copy(here, here, sem).wait()

    for i in range(1, n_expert):
        t = order(i)
        push(send.at[block(t)], got.at[at(0, e)], z_send.at[i - 1], recv.at[e], {"expert": t})
    got[at(0, e), :] = send[block(e), :]

    def arrived(k, s):
        landed(got.at[at(k, s)], recv.at[k * n_expert + s])

    def forward(i):
        s = order(i)
        arrived(1, s)
        arrived(2, s)
        if i % 2 == 0:
            push(got.at[at(1, s)], got.at[at(3, s)], f_send.at[i], recv.at[3 * n_expert + s], {"dp": yn})
        else:
            push(got.at[at(2, s)], got.at[at(3, s)], f_send.at[i], recv.at[3 * n_expert + s], {"dp": xn})

    lag = 2
    for i in range(n_expert):
        s = order(i)
        if i > 0:
            arrived(0, s)
        push(got.at[at(0, s)], got.at[at(1, s)], x_send.at[i], recv.at[n_expert + s], {"dp": xn})
        push(got.at[at(0, s)], got.at[at(2, s)], y_send.at[i], recv.at[2 * n_expert + s], {"dp": yn})
        if i >= lag:
            forward(i - lag)
    for load in loads[4:]:
        load.wait()

    tile = 256
    far = (1 - upper) * half
    near = upper * half
    spans = ((0, half + over), (half + over, half))

    def work(pieces, spilled, stops, between):
        mine = [pl.ds(pl.multiple_of(c * group + (near if j else far), half), half) for c, j in pieces]
        cut = half * len(pieces)
        if spilled:
            rest = pl.ds(spilled[0] * over, len(spilled) * over)
            tail = pl.ds(mains + spilled[0] * over, len(spilled) * over)
        for c in spilled:
            opened = pick(perm, got[pl.ds(c * group, group), 2 * width :])
            extra[pl.ds(c * over, over), :width] = unfold(opened, 0, width)
            extra[pl.ds(c * over, over), width:] = unfold(opened, LANES, width)

        def joined(main, more, cols):
            parts = [main[rows, cols] for rows in mine]
            return jnp.concatenate(parts + ([more[0][more[1], cols]] if spilled else []), axis=0)

        def spread(value, cols):
            for n, rows in enumerate(mine):
                ad[rows, cols] = value[n * half : (n + 1) * half]
            if spilled:
                ad[tail, cols] = value[cut:]

        more = (extra, rest) if spilled else None
        later_more = (ad, tail) if spilled else None

        def hidden(f):
            cols = pl.ds(pl.multiple_of(f * tile, tile), tile)
            later = pl.ds(pl.multiple_of(ff + f * tile, tile), tile)
            rows = joined(got, more, pl.ds(0, width))
            grads = joined(got, more, pl.ds(width, width))
            pre = jnp.dot(rows, first[:, cols], preferred_element_type=F32)
            act, slope = gelu_pair(pre)
            spread(act.astype(BF), cols)
            dact = lax.dot_general(
                grads, second[cols, :], (((1,), (1,)), ((), ())), preferred_element_type=F32
            )
            spread((dact * slope).astype(BF), later)

        low = 0
        for high, then in stops:
            pl.loop(low, high)(hidden)
            then()
            low = high
        pl.loop(low, ff // tile)(hidden)
        between()

        @pl.loop(0, width // tile)
        def _(f):
            cols = pl.ds(pl.multiple_of(f * tile, tile), tile)
            dpre = joined(ad, later_more, pl.ds(ff, ff))
            value = lax.dot_general(
                dpre, first[cols, :], (((1,), (1,)), ((), ())), preferred_element_type=F32
            ).astype(BF)
            for n, (c, j) in enumerate(pieces):
                part[pl.ds(c * chunk + spans[j][0], half), cols] = value[n * half : (n + 1) * half]
            for n, c in enumerate(spilled):
                part[pl.ds(c * chunk + half, over), cols] = value[cut + n * over : cut + (n + 1) * over]

    left, right = pl.ds(0, width // 2), pl.ds(width // 2, width // 2)

    def give(k, j, cols, dst, i, device):
        low, size = spans[j]
        push(
            part.at[pl.ds(k * chunk + low, size), cols],
            dst.at[pl.ds(low, size), cols],
            p_send.at[i],
            p_recv.at[i],
            {"dp": device},
        )

    def give_all(j):
        give(3, j, left, middle, 6 * j, xn)
        give(3, j, right, middle, 6 * j + 1, yn)
        give(1, j, left, peer_x, 6 * j + 2, xn)
        give(2, j, right, peer_y, 6 * j + 3, yn)

    def relay(j):
        low, size = spans[j]
        here = pl.ds(low, size)
        for k, cols, dst, device, m in ((2, left, peer_y, yn, 0), (1, right, peer_x, xn, 1)):
            mine = pl.ds(k * chunk + low, size)
            landed(middle.at[here, cols], p_recv.at[6 * j + m])
            value = part[mine, cols].astype(F32) + middle[here, cols].astype(F32)
            part[mine, cols] = value.astype(BF)
            give(k, j, cols, dst, 6 * j + 4 + m, device)

    def nothing():
        pass

    for i in range(n_expert // 2):
        arrived(3, order(i))
    stops = ((1, lambda: forward(n_expert - 2)), (2, lambda: forward(n_expert - 1)))
    work(((1, 1), (2, 1), (3, 1)), (), stops, nothing)
    give_all(1)
    for i in range(n_expert // 2, n_expert):
        arrived(3, order(i))
    work(((1, 0), (2, 0), (3, 0)), (1, 2, 3), (), lambda: relay(1))
    give_all(0)
    work(((0, 0), (0, 1)), (0,), (), nothing)
    relay(0)

    def weight_grad(left, left_at, right, right_at, grad, grad_hbm, sems):
        @pl.loop(0, width // tile)
        def _(f):
            cols = pl.ds(pl.multiple_of(left_at + f * tile, tile), tile)
            mine = pl.ds(pl.multiple_of(f * tile, tile), tile)
            tall = jnp.concatenate([left[0][pl.ds(0, mains), cols], left[1][left[2], cols]], axis=0)
            wide = jnp.concatenate(
                [
                    right[0][pl.ds(0, mains), right_at : right_at + width],
                    right[1][right[2], right_at : right_at + width],
                ],
                axis=0,
            )
            grad[mine, :] = lax.dot_general(
                tall, wide, (((0,), (0,)), ((), ())), preferred_element_type=F32
            )
            pltpu.make_async_copy(grad.at[mine], grad_hbm.at[mine], o_sem.at[sems + f]).start()

    def total(j):
        low, size = spans[j]
        here = pl.ds(low, size)
        landed(peer_x.at[here, left], p_recv.at[6 * j + 2])
        landed(peer_y.at[here, right], p_recv.at[6 * j + 3])
        landed(peer_y.at[here, left], p_recv.at[6 * j + 4])
        landed(peer_x.at[here, right], p_recv.at[6 * j + 5])
        value = part[here, :].astype(F32) + peer_x[here, :].astype(F32) + peer_y[here, :].astype(F32)
        return value.astype(BF)

    rows_all = (got, extra, pl.ds(0, 4 * over))
    hidden_all = (ad, ad, pl.ds(mains, 4 * over))
    near_rows = total(1)
    back_send[pl.ds(pl.multiple_of(near, half), half), :width] = near_rows
    weight_grad(hidden_all, 0, rows_all, width, grad_out, grad_out_out, 0)
    far_rows = total(0)
    back_send[pl.ds(pl.multiple_of(far, half), half), :width] = far_rows[:half]
    back_send[:, width:] = pick(perm, fold(far_rows[half:], width))

    def give_back(i):
        t = order(i)
        push(back_send.at[block(t)], back_got.at[block(e)], b_send.at[i - 1], b_recv.at[e], {"expert": t})

    for i in range(n_expert - 1, 0, -1):
        give_back(i)
    back_got[block(e), :] = back_send[block(e), :]

    weight_grad(rows_all, 0, hidden_all, ff, grad_in, grad_in_out, 4)

    for i in range(1, n_expert):
        s = order(i)
        landed(back_got.at[block(s)], b_recv.at[s])
    extra_rows = unfold(pick(perm, back_got[:, width:]), 0, width)
    spec = (((0,), (0,)), ((), ()))
    result = lax.dot_general(main_hot, back_got[:, :width], spec, preferred_element_type=F32)
    result = result + lax.dot_general(over_hot, extra_rows, spec, preferred_element_type=F32)
    out_ref[...] = result.astype(BF)
    for copy in started:
        copy.wait_send()
    for f in range(width // tile):
        mine = pl.ds(f * tile, tile)
        pltpu.make_async_copy(grad_out.at[mine], grad_out_out.at[mine], o_sem.at[f]).wait()
        pltpu.make_async_copy(grad_in.at[mine], grad_in_out.at[mine], o_sem.at[4 + f]).wait()


def deliver_kernel(small, first, second, small_out, first_out, second_out, sem):
    rows = first.shape[0] // 4
    copies = [pltpu.make_async_copy(small, small_out, sem.at[8])]
    for i in range(4):
        here = pl.ds(i * rows, rows)
        copies.append(pltpu.make_async_copy(first.at[here], first_out.at[here], sem.at[2 * i]))
        copies.append(pltpu.make_async_copy(second.at[here], second_out.at[here], sem.at[2 * i + 1]))
    for copy in copies:
        copy.start()
    for copy in copies:
        copy.wait()


def fused_body(tokens, upstream, task_ids, task_expert, w_in, w_out):
    n_expert = lax.axis_size("expert")
    rows_dev, width = tokens.shape
    ff = w_in.shape[2]
    group = n_expert * MAIN
    chunk = group + MAIN
    rows = 4 * chunk
    first, second = w_in[0], w_out[0]
    dma = pltpu.SemaphoreType.DMA
    vmem = pl.BlockSpec(memory_space=pltpu.VMEM)
    hbm = pl.BlockSpec(memory_space=pltpu.HBM)
    free = pl.BlockSpec(memory_space=pl.ANY)
    results = (
        jax.ShapeDtypeStruct((rows_dev, width), BF),
        jax.ShapeDtypeStruct((width, ff), F32),
        jax.ShapeDtypeStruct((ff, width), F32),
    )
    held = (tokens, upstream, task_ids.reshape(1, -1), task_expert, first, second)
    token_grad, grad_in, grad_out = pl.pallas_call(
        functools.partial(exchange_kernel, n_expert, rows_dev, width, ff),
        out_shape=results,
        in_specs=[hbm] * 6,
        out_specs=(vmem, free, free),
        scratch_shapes=[
            pltpu.VMEM((rows_dev, width), BF),
            pltpu.VMEM((rows_dev, width), BF),
            pltpu.VMEM((1, rows_dev), jnp.int32),
            pltpu.SMEM(task_expert.shape, jnp.int32),
            pltpu.VMEM((width, ff), BF),
            pltpu.VMEM((ff, width), BF),
            pltpu.VMEM((group, 2 * width + 2 * LANES), BF),
            pltpu.VMEM((4 * group, 2 * width + 2 * LANES), BF),
            pltpu.VMEM((4 * MAIN, 2 * width), BF),
            pltpu.VMEM((rows, 2 * ff), BF),
            pltpu.VMEM((rows, width), BF),
            pltpu.VMEM((chunk, width), BF),
            pltpu.VMEM((chunk, width), BF),
            pltpu.VMEM((chunk, width), BF),
            pltpu.VMEM((width, ff), F32),
            pltpu.VMEM((ff, width), F32),
            pltpu.VMEM((group, width + LANES), BF),
            pltpu.VMEM((group, width + LANES), BF),
            dma((6,)),
            dma((n_expert - 1,)),
            dma((n_expert,)),
            dma((n_expert,)),
            dma((n_expert,)),
            dma((4 * n_expert,)),
            dma((12,)),
            dma((12,)),
            dma((n_expert - 1,)),
            dma((n_expert,)),
            dma((8,)),
        ],
        compiler_params=pltpu.CompilerParams(
            collective_id=0, has_side_effects=True, vmem_limit_bytes=40 * 1024 * 1024
        ),
        cost_estimate=pl.CostEstimate(
            flops=10 * rows * width * ff, bytes_accessed=12 * width * ff, transcendentals=rows * ff
        ),
    )(*(pltpu.with_memory_space_constraint(x, pltpu.HBM) for x in held))
    token_grad, grad_in, grad_out = pl.pallas_call(
        deliver_kernel,
        out_shape=results,
        in_specs=[free, free, free],
        out_specs=(free, free, free),
        scratch_shapes=[dma((9,))],
        compiler_params=pltpu.CompilerParams(vmem_limit_bytes=1024 * 1024),
        cost_estimate=pl.CostEstimate(flops=0, bytes_accessed=16 * width * ff, transcendentals=0),
    )(token_grad, grad_in, grad_out)
    return (token_grad, grad_in[None], grad_out[None])


def general_body(tokens, upstream, task_ids, task_expert, w_in, w_out):
    n_expert = lax.axis_size("expert")
    rows_dev = tokens.shape[0]
    width = tokens.shape[1]
    experts = task_expert.shape[0]
    capacity = max(2, (9 * rows_dev // 8 + n_expert - 1) // n_expert)
    lanes = jnp.arange(experts, dtype=jnp.int32)
    task_hot = (task_ids == lanes[None, :]).astype(jnp.int32)
    target = jnp.sum(task_hot * task_expert[None, :], axis=1)
    dest_hot = (target[:, None] == lanes[None, :]).astype(jnp.int32)
    before = jnp.cumsum(dest_hot, axis=0) - dest_hot
    rank = jnp.sum(before * dest_hot, axis=1)
    slot = target * capacity + rank
    packer = (jnp.arange(experts * capacity, dtype=jnp.int32)[:, None] == slot[None, :]).astype(
        jnp.bfloat16
    )
    send_rows = (
        jnp.dot(packer, tokens, preferred_element_type=jnp.float32)
        .astype(jnp.bfloat16)
        .reshape(experts, capacity, width)
    )
    send_grads = (
        jnp.dot(packer, upstream, preferred_element_type=jnp.float32)
        .astype(jnp.bfloat16)
        .reshape(experts, capacity, width)
    )
    first = w_in[0]
    second = w_out[0]
    got_rows, got_grads = (
        lax.all_to_all(send_rows, "expert", split_axis=0, concat_axis=0, tiled=True),
        lax.all_to_all(send_grads, "expert", split_axis=0, concat_axis=0, tiled=True),
    )
    got_rows = got_rows.reshape(experts * capacity, width)
    got_grads = got_grads.reshape(experts * capacity, width)
    all_rows, all_grads = (
        lax.all_gather(got_rows, "dp", axis=0, tiled=True),
        lax.all_gather(got_grads, "dp", axis=0, tiled=True),
    )
    pre = jnp.dot(all_rows, first, preferred_element_type=jnp.float32)
    act, slope = gelu_pair(pre)
    act = act.astype(jnp.bfloat16)
    grad_second = lax.dot_general(
        act, all_grads, (((0,), (0,)), ((), ())), preferred_element_type=jnp.float32
    )
    dact = lax.dot_general(
        all_grads, second, (((1,), (1,)), ((), ())), preferred_element_type=jnp.float32
    )
    dpre = (dact * slope).astype(jnp.bfloat16)
    grad_first = lax.dot_general(
        all_rows, dpre, (((0,), (0,)), ((), ())), preferred_element_type=jnp.float32
    )
    partial_value = lax.dot_general(
        dpre, first, (((1,), (1,)), ((), ())), preferred_element_type=jnp.float32
    )
    own = lax.psum_scatter(
        partial_value.astype(jnp.bfloat16), "dp", scatter_dimension=0, tiled=True
    ).astype(jnp.float32)
    own = own.astype(jnp.bfloat16).reshape(experts, capacity, width)
    back = lax.all_to_all(own, "expert", split_axis=0, concat_axis=0, tiled=True).reshape(
        experts * capacity, width
    )
    token_grad = lax.dot_general(
        packer, back, (((0,), (0,)), ((), ())), preferred_element_type=jnp.float32
    ).astype(jnp.bfloat16)
    return (token_grad, grad_first[None], grad_second[None])


def body(mesh, tokens, upstream, task_ids, task_expert, w_in, w_out):
    n_expert = mesh.shape["expert"]
    rows_dev, width = tokens.shape
    ff = w_in.shape[2]
    capacity = max(2, (9 * rows_dev // 8 + n_expert - 1) // n_expert)
    fits = (
        mesh.shape["dp"] == 4
        and n_expert == 8
        and rows_dev == 128
        and capacity <= MAIN + 2
        and width == n_expert * LANES
        and ff == width
    )
    run = fused_body if fits else general_body
    return run(tokens, upstream, task_ids, task_expert, w_in, w_out)


def solution(mesh):
    placed = (
        P(("dp", "expert"), None),
        P(("dp", "expert"), None),
        P(("dp", "expert"), None),
        P(),
        P("expert", None, "dp"),
        P("expert", "dp", None),
    )
    return jax.shard_map(
        functools.partial(body, mesh),
        mesh=mesh,
        in_specs=placed,
        out_specs=(P(("dp", "expert"), None), P("expert", None, "dp"), P("expert", "dp", None)),
        check_vma=False,
    )
```

```python
import functools

import jax
import jax.numpy as jnp
from jax import lax
from jax.experimental import pallas as pl
from jax.experimental.pallas import tpu as pltpu
from jax.sharding import PartitionSpec as P

coeff = 0.7978845608028654
MESH = pl.DeviceIdType.MESH
BF = jnp.bfloat16
F32 = jnp.float32
MAIN = 16
LANES = 128


def gelu_pair(pre):
    square = pre * pre
    tanh_val = jnp.tanh(pre * (coeff + coeff * 0.044715 * square))
    half = 0.5 + 0.5 * tanh_val
    slope = half + half * (1.0 - tanh_val) * (pre * (coeff + 3.0 * 0.044715 * coeff * square))
    return (pre * half, slope)


def fold(rows, width):
    return jnp.concatenate([rows[:, c : c + LANES] for c in range(0, width, LANES)], axis=0)


def unfold(rows, start, width):
    return jnp.concatenate(
        [rows[c * MAIN : (c + 1) * MAIN, start : start + LANES] for c in range(width // LANES)], axis=1
    )


def exchange_kernel(
    n_expert,
    rows_dev,
    width,
    ff,
    tokens_hbm,
    upstream_hbm,
    ids_hbm,
    experts_hbm,
    first_hbm,
    second_hbm,
    out_ref,
    grad_in_out,
    grad_out_out,
    tokens_ref,
    upstream_ref,
    ids_ref,
    experts_ref,
    first,
    second,
    send,
    got,
    extra,
    ad,
    part,
    middle,
    peer_x,
    peer_y,
    grad_in,
    grad_out,
    back_send,
    back_got,
    w_sem,
    z_send,
    x_send,
    y_send,
    f_send,
    recv,
    p_send,
    p_recv,
    b_send,
    b_recv,
    o_sem,
):
    chips = n_expert // 2
    group = n_expert * MAIN
    over = MAIN
    half = group // 2
    chunk = group + over
    mains = 4 * group
    e = lax.axis_index("expert")
    d = lax.axis_index("dp")
    chip, core = lax.div(e, 2), lax.rem(e, 2)
    xn = d + 1 - 2 * lax.rem(d, 2)
    yn = lax.rem(d + 2, 4)
    diag = lax.rem(xn + 2, 4)
    upper = lax.div(chip, chips // 2)
    inner = chip + upper * (chips - 1 - 2 * chip)

    def order(i):
        place = (inner, 1 - inner, 2, 3)[i // 2]
        return (place + upper * (chips - 1 - 2 * place)) * 2 + lax.rem(core + i % 2, 2)

    def block(index):
        return pl.ds(pl.multiple_of(index * MAIN, MAIN), MAIN)

    def at(k, s):
        return pl.ds(pl.multiple_of(k * group + s * MAIN, MAIN), MAIN)

    loads = [
        pltpu.make_async_copy(src, dst, w_sem.at[i])
        for i, (src, dst) in enumerate(
            (
                (ids_hbm, ids_ref),
                (experts_hbm, experts_ref),
                (tokens_hbm, tokens_ref),
                (upstream_hbm, upstream_ref),
                (first_hbm, first),
                (second_hbm, second),
            )
        )
    ]
    for load in loads:
        load.start()

    barrier = pltpu.get_barrier_semaphore()
    for i in range(1, n_expert):
        pl.semaphore_signal(barrier, inc=1, device_id={"expert": order(i)}, device_id_type=MESH)
    for near in (xn, yn, diag):
        pl.semaphore_signal(barrier, inc=1, device_id={"dp": near}, device_id_type=MESH)

    row = lax.broadcasted_iota(jnp.int32, (rows_dev, rows_dev), 0)
    col = lax.broadcasted_iota(jnp.int32, (rows_dev, rows_dev), 1)
    line = row.astype(F32)
    earlier = (row < col).astype(BF)
    turned = (row >> 1 & 7) * 16 + (row >> 4) * 2 + (row & 1)
    perm = (turned == col).astype(BF)
    loads[0].wait()
    loads[1].wait()
    ids = ids_ref[...]
    goal = jnp.zeros(ids.shape, F32)
    for k in range(n_expert):
        goal = jnp.where(ids == k, experts_ref[k].astype(F32), goal)
    dest = (goal == line).astype(F32)
    before = jnp.dot(dest.astype(BF), earlier, preferred_element_type=F32)
    rank = jnp.sum(before * dest, axis=0, keepdims=True)
    is_main = (rank < MAIN).astype(F32)
    main_hot = ((goal * MAIN + rank == line).astype(F32) * is_main).astype(BF)
    over_hot = ((goal * 2 + (rank - MAIN) == line).astype(F32) * (1.0 - is_main)).astype(BF)[:over]

    def pick(hot_rows, values):
        return jnp.dot(hot_rows, values, preferred_element_type=F32).astype(BF)

    loads[2].wait()
    tokens = tokens_ref[...]
    send[:, :width] = pick(main_hot, tokens)
    loads[3].wait()
    upstream = upstream_ref[...]
    send[:, width : 2 * width] = pick(main_hot, upstream)
    folded = jnp.concatenate(
        [fold(pick(over_hot, tokens), width), fold(pick(over_hot, upstream), width)], axis=1
    )
    send[:, 2 * width :] = pick(perm, folded)

    pl.semaphore_wait(barrier, n_expert - 1 + 3)

    started = []

    def push(src, dst, send_sem, recv_sem, device):
        copy = pltpu.make_async_remote_copy(
            src_ref=src,
            dst_ref=dst,
            send_sem=send_sem,
            recv_sem=recv_sem,
            device_id=device,
            device_id_type=MESH,
        )
        copy.start()
        started.append(copy)

    def landed(here, sem):
        pltpu.make_async_copy(here, here, sem).wait()

    push(send.at[block(e)], got.at[at(1, e)], x_send.at[0], recv.at[n_expert + e], {"dp": xn})
    push(send.at[block(e)], got.at[at(2, e)], y_send.at[0], recv.at[2 * n_expert + e], {"dp": yn})
    for i in range(1, n_expert):
        t = order(i)
        push(send.at[block(t)], got.at[at(0, e)], z_send.at[i - 1], recv.at[e], {"expert": t})
    got[at(0, e), :] = send[block(e), :]

    def arrived(k, s):
        landed(got.at[at(k, s)], recv.at[k * n_expert + s])

    def forward(i):
        s = order(i)
        arrived(1, s)
        arrived(2, s)
        if i % 2 == 0:
            push(got.at[at(1, s)], got.at[at(3, s)], f_send.at[i], recv.at[3 * n_expert + s], {"dp": yn})
        else:
            push(got.at[at(2, s)], got.at[at(3, s)], f_send.at[i], recv.at[3 * n_expert + s], {"dp": xn})

    lag = 2
    for i in range(1, n_expert):
        s = order(i)
        arrived(0, s)
        push(got.at[at(0, s)], got.at[at(1, s)], x_send.at[i], recv.at[n_expert + s], {"dp": xn})
        push(got.at[at(0, s)], got.at[at(2, s)], y_send.at[i], recv.at[2 * n_expert + s], {"dp": yn})
        if i >= lag:
            forward(i - lag)
    for load in loads[4:]:
        load.wait()

    tile = 256
    far = (1 - upper) * half
    near = upper * half
    spans = ((0, half + over), (half + over, half))

    def work(pieces, spilled, stops, between):
        mine = [pl.ds(pl.multiple_of(c * group + (near if j else far), half), half) for c, j in pieces]
        cut = half * len(pieces)
        if spilled:
            rest = pl.ds(spilled[0] * over, len(spilled) * over)
            tail = pl.ds(mains + spilled[0] * over, len(spilled) * over)
        for c in spilled:
            opened = pick(perm, got[pl.ds(c * group, group), 2 * width :])
            extra[pl.ds(c * over, over), :width] = unfold(opened, 0, width)
            extra[pl.ds(c * over, over), width:] = unfold(opened, LANES, width)

        def joined(main, more, cols):
            parts = [main[rows, cols] for rows in mine]
            return jnp.concatenate(parts + ([more[0][more[1], cols]] if spilled else []), axis=0)

        def spread(value, cols):
            for n, rows in enumerate(mine):
                ad[rows, cols] = value[n * half : (n + 1) * half]
            if spilled:
                ad[tail, cols] = value[cut:]

        more = (extra, rest) if spilled else None
        later_more = (ad, tail) if spilled else None

        def hidden(f):
            cols = pl.ds(pl.multiple_of(f * tile, tile), tile)
            later = pl.ds(pl.multiple_of(ff + f * tile, tile), tile)
            rows = joined(got, more, pl.ds(0, width))
            grads = joined(got, more, pl.ds(width, width))
            pre = jnp.dot(rows, first[:, cols], preferred_element_type=F32)
            act, slope = gelu_pair(pre)
            spread(act.astype(BF), cols)
            dact = lax.dot_general(
                grads, second[cols, :], (((1,), (1,)), ((), ())), preferred_element_type=F32
            )
            spread((dact * slope).astype(BF), later)

        low = 0
        for high, then in stops:
            pl.loop(low, high)(hidden)
            then()
            low = high
        pl.loop(low, ff // tile)(hidden)
        between()

        @pl.loop(0, width // tile)
        def _(f):
            cols = pl.ds(pl.multiple_of(f * tile, tile), tile)
            dpre = joined(ad, later_more, pl.ds(ff, ff))
            value = lax.dot_general(
                dpre, first[cols, :], (((1,), (1,)), ((), ())), preferred_element_type=F32
            ).astype(BF)
            for n, (c, j) in enumerate(pieces):
                part[pl.ds(c * chunk + spans[j][0], half), cols] = value[n * half : (n + 1) * half]
            for n, c in enumerate(spilled):
                part[pl.ds(c * chunk + half, over), cols] = value[cut + n * over : cut + (n + 1) * over]

    left, right = pl.ds(0, width // 2), pl.ds(width // 2, width // 2)

    def give(k, j, cols, dst, i, device):
        low, size = spans[j]
        push(
            part.at[pl.ds(k * chunk + low, size), cols],
            dst.at[pl.ds(low, size), cols],
            p_send.at[i],
            p_recv.at[i],
            {"dp": device},
        )

    def give_all(j):
        give(3, j, left, middle, 6 * j, xn)
        give(3, j, right, middle, 6 * j + 1, yn)
        give(1, j, left, peer_x, 6 * j + 2, xn)
        give(2, j, right, peer_y, 6 * j + 3, yn)

    def relay(j):
        low, size = spans[j]
        here = pl.ds(low, size)
        for k, cols, dst, device, m in ((2, left, peer_y, yn, 0), (1, right, peer_x, xn, 1)):
            mine = pl.ds(k * chunk + low, size)
            landed(middle.at[here, cols], p_recv.at[6 * j + m])
            value = part[mine, cols].astype(F32) + middle[here, cols].astype(F32)
            part[mine, cols] = value.astype(BF)
            give(k, j, cols, dst, 6 * j + 4 + m, device)

    def nothing():
        pass

    for i in range(n_expert // 2):
        arrived(3, order(i))
    stops = ((1, lambda: forward(n_expert - 2)), (2, lambda: forward(n_expert - 1)))
    work(((1, 1), (2, 1), (3, 1)), (), stops, nothing)
    give_all(1)
    for i in range(n_expert // 2, n_expert):
        arrived(3, order(i))
    work(((1, 0), (2, 0), (3, 0)), (1, 2, 3), (), lambda: relay(1))
    give_all(0)
    work(((0, 0), (0, 1)), (0,), (), nothing)
    relay(0)

    def weight_grad(left, left_at, right, right_at, grad, grad_hbm, sems):
        @pl.loop(0, width // tile)
        def _(f):
            cols = pl.ds(pl.multiple_of(left_at + f * tile, tile), tile)
            mine = pl.ds(pl.multiple_of(f * tile, tile), tile)
            tall = jnp.concatenate([left[0][pl.ds(0, mains), cols], left[1][left[2], cols]], axis=0)
            wide = jnp.concatenate(
                [
                    right[0][pl.ds(0, mains), right_at : right_at + width],
                    right[1][right[2], right_at : right_at + width],
                ],
                axis=0,
            )
            grad[mine, :] = lax.dot_general(
                tall, wide, (((0,), (0,)), ((), ())), preferred_element_type=F32
            )
            pltpu.make_async_copy(grad.at[mine], grad_hbm.at[mine], o_sem.at[sems + f]).start()

    def total(j):
        low, size = spans[j]
        here = pl.ds(low, size)
        landed(peer_x.at[here, left], p_recv.at[6 * j + 2])
        landed(peer_y.at[here, right], p_recv.at[6 * j + 3])
        landed(peer_y.at[here, left], p_recv.at[6 * j + 4])
        landed(peer_x.at[here, right], p_recv.at[6 * j + 5])
        value = part[here, :].astype(F32) + peer_x[here, :].astype(F32) + peer_y[here, :].astype(F32)
        return value.astype(BF)

    rows_all = (got, extra, pl.ds(0, 4 * over))
    hidden_all = (ad, ad, pl.ds(mains, 4 * over))
    near_rows = total(1)
    back_send[pl.ds(pl.multiple_of(near, half), half), :width] = near_rows
    weight_grad(hidden_all, 0, rows_all, width, grad_out, grad_out_out, 0)
    far_rows = total(0)
    back_send[pl.ds(pl.multiple_of(far, half), half), :width] = far_rows[:half]
    back_send[:, width:] = pick(perm, fold(far_rows[half:], width))

    def give_back(i):
        t = order(i)
        push(back_send.at[block(t)], back_got.at[block(e)], b_send.at[i - 1], b_recv.at[e], {"expert": t})

    for i in range(n_expert - 1, 0, -1):
        give_back(i)
    back_got[block(e), :] = back_send[block(e), :]

    weight_grad(rows_all, 0, hidden_all, ff, grad_in, grad_in_out, 4)

    for i in range(1, n_expert):
        s = order(i)
        landed(back_got.at[block(s)], b_recv.at[s])
    extra_rows = unfold(pick(perm, back_got[:, width:]), 0, width)
    spec = (((0,), (0,)), ((), ()))
    result = lax.dot_general(main_hot, back_got[:, :width], spec, preferred_element_type=F32)
    result = result + lax.dot_general(over_hot, extra_rows, spec, preferred_element_type=F32)
    out_ref[...] = result.astype(BF)
    for copy in started:
        copy.wait_send()
    for f in range(width // tile):
        mine = pl.ds(f * tile, tile)
        pltpu.make_async_copy(grad_out.at[mine], grad_out_out.at[mine], o_sem.at[f]).wait()
        pltpu.make_async_copy(grad_in.at[mine], grad_in_out.at[mine], o_sem.at[4 + f]).wait()


def deliver_kernel(small, first, second, small_out, first_out, second_out, sem):
    rows = first.shape[0] // 4
    copies = [pltpu.make_async_copy(small, small_out, sem.at[8])]
    for i in range(4):
        here = pl.ds(i * rows, rows)
        copies.append(pltpu.make_async_copy(first.at[here], first_out.at[here], sem.at[2 * i]))
        copies.append(pltpu.make_async_copy(second.at[here], second_out.at[here], sem.at[2 * i + 1]))
    for copy in copies:
        copy.start()
    for copy in copies:
        copy.wait()


def fused_body(tokens, upstream, task_ids, task_expert, w_in, w_out):
    n_expert = lax.axis_size("expert")
    rows_dev, width = tokens.shape
    ff = w_in.shape[2]
    group = n_expert * MAIN
    chunk = group + MAIN
    rows = 4 * chunk
    first, second = w_in[0], w_out[0]
    dma = pltpu.SemaphoreType.DMA
    vmem = pl.BlockSpec(memory_space=pltpu.VMEM)
    hbm = pl.BlockSpec(memory_space=pltpu.HBM)
    free = pl.BlockSpec(memory_space=pl.ANY)
    results = (
        jax.ShapeDtypeStruct((rows_dev, width), BF),
        jax.ShapeDtypeStruct((width, ff), F32),
        jax.ShapeDtypeStruct((ff, width), F32),
    )
    held = (tokens, upstream, task_ids.reshape(1, -1), task_expert, first, second)
    token_grad, grad_in, grad_out = pl.pallas_call(
        functools.partial(exchange_kernel, n_expert, rows_dev, width, ff),
        out_shape=results,
        in_specs=[hbm] * 6,
        out_specs=(vmem, free, free),
        scratch_shapes=[
            pltpu.VMEM((rows_dev, width), BF),
            pltpu.VMEM((rows_dev, width), BF),
            pltpu.VMEM((1, rows_dev), jnp.int32),
            pltpu.SMEM(task_expert.shape, jnp.int32),
            pltpu.VMEM((width, ff), BF),
            pltpu.VMEM((ff, width), BF),
            pltpu.VMEM((group, 2 * width + 2 * LANES), BF),
            pltpu.VMEM((4 * group, 2 * width + 2 * LANES), BF),
            pltpu.VMEM((4 * MAIN, 2 * width), BF),
            pltpu.VMEM((rows, 2 * ff), BF),
            pltpu.VMEM((rows, width), BF),
            pltpu.VMEM((chunk, width), BF),
            pltpu.VMEM((chunk, width), BF),
            pltpu.VMEM((chunk, width), BF),
            pltpu.VMEM((width, ff), F32),
            pltpu.VMEM((ff, width), F32),
            pltpu.VMEM((group, width + LANES), BF),
            pltpu.VMEM((group, width + LANES), BF),
            dma((6,)),
            dma((n_expert - 1,)),
            dma((n_expert,)),
            dma((n_expert,)),
            dma((n_expert,)),
            dma((4 * n_expert,)),
            dma((12,)),
            dma((12,)),
            dma((n_expert - 1,)),
            dma((n_expert,)),
            dma((8,)),
        ],
        compiler_params=pltpu.CompilerParams(
            collective_id=0, has_side_effects=True, vmem_limit_bytes=40 * 1024 * 1024
        ),
        cost_estimate=pl.CostEstimate(
            flops=10 * rows * width * ff, bytes_accessed=12 * width * ff, transcendentals=rows * ff
        ),
    )(*(pltpu.with_memory_space_constraint(x, pltpu.HBM) for x in held))
    token_grad, grad_in, grad_out = pl.pallas_call(
        deliver_kernel,
        out_shape=results,
        in_specs=[free, free, free],
        out_specs=(free, free, free),
        scratch_shapes=[dma((9,))],
        compiler_params=pltpu.CompilerParams(vmem_limit_bytes=1024 * 1024),
        cost_estimate=pl.CostEstimate(flops=0, bytes_accessed=16 * width * ff, transcendentals=0),
    )(token_grad, grad_in, grad_out)
    return (token_grad, grad_in[None], grad_out[None])


def general_body(tokens, upstream, task_ids, task_expert, w_in, w_out):
    n_expert = lax.axis_size("expert")
    rows_dev = tokens.shape[0]
    width = tokens.shape[1]
    experts = task_expert.shape[0]
    capacity = max(2, (9 * rows_dev // 8 + n_expert - 1) // n_expert)
    lanes = jnp.arange(experts, dtype=jnp.int32)
    task_hot = (task_ids == lanes[None, :]).astype(jnp.int32)
    target = jnp.sum(task_hot * task_expert[None, :], axis=1)
    dest_hot = (target[:, None] == lanes[None, :]).astype(jnp.int32)
    before = jnp.cumsum(dest_hot, axis=0) - dest_hot
    rank = jnp.sum(before * dest_hot, axis=1)
    slot = target * capacity + rank
    packer = (jnp.arange(experts * capacity, dtype=jnp.int32)[:, None] == slot[None, :]).astype(
        jnp.bfloat16
    )
    send_rows = (
        jnp.dot(packer, tokens, preferred_element_type=jnp.float32)
        .astype(jnp.bfloat16)
        .reshape(experts, capacity, width)
    )
    send_grads = (
        jnp.dot(packer, upstream, preferred_element_type=jnp.float32)
        .astype(jnp.bfloat16)
        .reshape(experts, capacity, width)
    )
    first = w_in[0]
    second = w_out[0]
    got_rows, got_grads = (
        lax.all_to_all(send_rows, "expert", split_axis=0, concat_axis=0, tiled=True),
        lax.all_to_all(send_grads, "expert", split_axis=0, concat_axis=0, tiled=True),
    )
    got_rows = got_rows.reshape(experts * capacity, width)
    got_grads = got_grads.reshape(experts * capacity, width)
    all_rows, all_grads = (
        lax.all_gather(got_rows, "dp", axis=0, tiled=True),
        lax.all_gather(got_grads, "dp", axis=0, tiled=True),
    )
    pre = jnp.dot(all_rows, first, preferred_element_type=jnp.float32)
    act, slope = gelu_pair(pre)
    act = act.astype(jnp.bfloat16)
    grad_second = lax.dot_general(
        act, all_grads, (((0,), (0,)), ((), ())), preferred_element_type=jnp.float32
    )
    dact = lax.dot_general(
        all_grads, second, (((1,), (1,)), ((), ())), preferred_element_type=jnp.float32
    )
    dpre = (dact * slope).astype(jnp.bfloat16)
    grad_first = lax.dot_general(
        all_rows, dpre, (((0,), (0,)), ((), ())), preferred_element_type=jnp.float32
    )
    partial_value = lax.dot_general(
        dpre, first, (((1,), (1,)), ((), ())), preferred_element_type=jnp.float32
    )
    own = lax.psum_scatter(
        partial_value.astype(jnp.bfloat16), "dp", scatter_dimension=0, tiled=True
    ).astype(jnp.float32)
    own = own.astype(jnp.bfloat16).reshape(experts, capacity, width)
    back = lax.all_to_all(own, "expert", split_axis=0, concat_axis=0, tiled=True).reshape(
        experts * capacity, width
    )
    token_grad = lax.dot_general(
        packer, back, (((0,), (0,)), ((), ())), preferred_element_type=jnp.float32
    ).astype(jnp.bfloat16)
    return (token_grad, grad_first[None], grad_second[None])


def body(mesh, tokens, upstream, task_ids, task_expert, w_in, w_out):
    n_expert = mesh.shape["expert"]
    rows_dev, width = tokens.shape
    ff = w_in.shape[2]
    capacity = max(2, (9 * rows_dev // 8 + n_expert - 1) // n_expert)
    fits = (
        mesh.shape["dp"] == 4
        and n_expert == 8
        and rows_dev == 128
        and capacity <= MAIN + 2
        and width == n_expert * LANES
        and ff == width
    )
    run = fused_body if fits else general_body
    return run(tokens, upstream, task_ids, task_expert, w_in, w_out)


def solution(mesh):
    placed = (
        P(("dp", "expert"), None),
        P(("dp", "expert"), None),
        P(("dp", "expert"), None),
        P(),
        P("expert", None, "dp"),
        P("expert", "dp", None),
    )
    return jax.shard_map(
        functools.partial(body, mesh),
        mesh=mesh,
        in_specs=placed,
        out_specs=(P(("dp", "expert"), None), P("expert", None, "dp"), P("expert", "dp", None)),
        check_vma=False,
    )
```
